32 devices in a mesh: pos: 16 (over z, y, x), val: 2 (over core).
Axes of the slice: x: 2, y: 2, z: 4, core: 2. Of those that a mesh axis runs over, the one named last changes fastest.
Arguments:
- send_load: int32 [2, 16], replicated, may hold values from 1 to 16, 64 in all within a row
- tokens: int32 [2, 256, 81], P('val', 'pos'), may hold values from 0 to 63
- owner: int32 [2, 256], P('val', 'pos'), may hold values from 0 to 15
- joint_action: int32 [2, 256, 7], P('val', 'pos'), may hold values from 0 to 31
- board_context: bfloat16 [32, 81, 512], P('pos'), may hold values from -6 to 6
- tok_embed: bfloat16 [64, 512], replicated, may hold values from -6 to 6
- w_qkv: bfloat16 [512, 1536], replicated, may hold values from -0.25 to 0.25
- w_attn_out: bfloat16 [512, 512], replicated, may hold values from -0.25 to 0.25
- w_up: bfloat16 [512, 1024], replicated, may hold values from -0.25 to 0.25
- w_down: bfloat16 [1024, 512], replicated, may hold values from -0.1875 to 0.1875
- w_value: bfloat16 [512, 7], replicated, may hold values from -0.25 to 0.25
Outputs:
- state_values: float32 [2, 256, 7], P('val', 'pos')
- avg_policy: float32 [32, 7, 32], P('pos')
The draws below stay inside these ranges and needn't reach their ends.
Inputs may be any that keep to these rules, and one draw needn't show every extreme that they name: Each row of send_load sums to 64, and its largest entry is exactly 16.
All inputs are finite; a program needn't handle non-finite values.
Results may differ from the reference program's by a relative error of at most 0.0055.
Values may be sent and summed in bfloat16 or wider, within the bound.
No kernel may reach another device: no remote copies, remote signals or barrier semaphores. Data moves between devices by JAX's collectives and lax.ppermute only.
A program may use at most 64 MiB of HBM per device.

```python
import math
import jax
import jax.numpy as jnp
import numpy as np
from jax import lax

D = 512
HEADS = 8
FF = 1024
LOCS = 81
VOCAB = 64
POWERS = 7
ACTIONS = 32
ITERS = 8
P_DEV = 2
LMAX = 16
EVAL = 4
SLOTS = 256
POSITIONS = 32
N_POS = 16
N_VAL = 2


def touch_ends(entries, own_key, smallest, largest):
    shape = entries.shape
    index_at = [jax.random.randint(jax.random.fold_in(own_key, axis), (), 0, shape[axis]) for axis in range(len(shape))]
    entries = entries.at[tuple(index_at)].set(smallest)
    longest = shape.index(max(shape))
    index_at[longest] = (index_at[longest] + 1) % shape[longest]
    return entries.at[tuple(index_at)].set(largest)


def level_of(key, shape, shards, low, top_value):
    def one(dim, parts):
        draws = jax.random.uniform(jax.random.fold_in(jax.random.fold_in(key, 6), dim), (parts,), jnp.float32, low / len(shards), top_value / len(shards))
        return jnp.repeat(jnp.exp(draws), shape[dim] // parts).reshape((-1,) + (1,) * (len(shape) - dim - 1))

    gain = one(*shards[0])
    for cut in shards[1:]:
        gain = gain * one(*cut)
    return gain


def split_up(count, total, limit, skew):
    loads = [(1 << 20) // math.isqrt(standing ** skew) + 1 for standing in range(2, count + 1)]
    surplus, holding = total - limit - (count - 1), [1] * (count - 1)
    while surplus > 0:
        free = [i for i in range(count - 1) if holding[i] < limit]
        pool, remaining = sum([loads[i] for i in free]), surplus
        for i in free:
            extra = min(limit - holding[i], max(1, remaining * loads[i] // pool), surplus)
            holding[i] = holding[i] + extra
            surplus = surplus - extra
    return np.array([limit] + holding)


def uneven_parts(rng, count, total, reach, slope):
    if count == 2:
        one = jax.random.randint(rng, (), max(1, total - reach), min(reach, total - 1) + 1)
        return jnp.stack([one, total - one])
    sizes = jnp.asarray(split_up(count, total, reach, slope), jnp.int32)
    pairs = (count - 1) // 2
    giver, sink = sizes[1:1 + 2 * pairs:2], sizes[2:2 + 2 * pairs:2]
    slack = jnp.minimum(giver - 1, reach - sink)
    shifted = jax.random.randint(jax.random.fold_in(rng, 1), (pairs,), 0, 1 << 20) % (slack + 1)
    sizes = sizes.at[1:1 + 2 * pairs:2].set(giver - shifted).at[2:2 + 2 * pairs:2].set(sink + shifted)
    return sizes[jax.random.permutation(jax.random.fold_in(rng, 2), count)]


def normal_values(own_key, extent, scale, bound, shards=(), kind=jnp.bfloat16):
    result = jax.random.normal(own_key, extent, jnp.float32) * scale
    if len(shards) > 0:
        result = level_of(own_key, extent, shards, -0.22, 0.18) * result
    return jnp.clip(result, min=-bound, max=bound).astype(kind)


def setup_inputs(seed: int = 0) -> dict:
    streams_of = jax.random.split(jax.random.key(seed), 12)
    return {
        "send_load": jax.vmap(lambda own: uneven_parts(own, N_POS, N_POS * EVAL, LMAX, 2))(jax.random.split(streams_of[0], N_VAL)).reshape((N_VAL, N_POS)).astype(jnp.int32),
        "tokens": touch_ends(jax.random.randint(streams_of[1], (N_VAL, SLOTS, LOCS), 0, VOCAB), jax.random.fold_in(streams_of[1], 1), 0, VOCAB - 1).astype(jnp.int32),
        "owner": touch_ends(jax.random.randint(streams_of[2], (N_VAL, SLOTS), 0, P_DEV * ITERS), jax.random.fold_in(streams_of[2], 1), 0, (P_DEV * ITERS) - 1).astype(jnp.int32),
        "joint_action": touch_ends(jax.random.randint(streams_of[3], (N_VAL, SLOTS, POWERS), 0, ACTIONS), jax.random.fold_in(streams_of[3], 1), 0, ACTIONS - 1).astype(jnp.int32),
        "board_context": normal_values(streams_of[4], (POSITIONS, LOCS, D), 1.0, 6.0, ((0, 16),)),
        "tok_embed": normal_values(streams_of[5], (VOCAB, D), 1.0, 6.0),
        "w_qkv": normal_values(streams_of[6], (D, 3 * D), D ** -0.5, 0.25),
        "w_attn_out": normal_values(streams_of[7], (D, D), D ** -0.5, 0.25),
        "w_up": normal_values(streams_of[8], (D, FF), D ** -0.5, 0.25),
        "w_down": normal_values(streams_of[9], (FF, D), FF ** -0.5, 0.1875),
        "w_value": normal_values(streams_of[10], (D, POWERS), D ** -0.5, 0.25),
    }


smoothing = 0.01

def layer_norm(values):
    centre = values - lax.optimization_barrier(jnp.mean(values, axis=-1, keepdims=True))
    spread = lax.optimization_barrier(jnp.mean(centre * centre, axis=-1, keepdims=True))
    return centre * lax.rsqrt(spread + 1e-05)

def multiply(pattern, first_op, second_op):
    return jnp.einsum(pattern, first_op.astype(jnp.float32), second_op.astype(jnp.float32), precision=lax.Precision.HIGHEST)

def encode(states, w_qkv, w_attn_out, w_up, w_down, w_value):
    batch_size, loc_count, model_width = states.shape
    head_size = model_width // HEADS
    inputs = states.astype(jnp.float32)
    normed = layer_norm(inputs).astype(jnp.bfloat16)
    joined = multiply('bld,de->ble', normed, w_qkv).astype(jnp.bfloat16)
    queries = joined[:, :, :model_width].reshape(batch_size, loc_count, HEADS, head_size)
    key_rows = joined[:, :, model_width:2 * model_width].reshape(batch_size, loc_count, HEADS, head_size)
    value_rows = joined[:, :, 2 * model_width:].reshape(batch_size, loc_count, HEADS, head_size)
    scores = multiply('bqhe,bkhe->bhqk', queries, key_rows) * head_size ** (-0.5)
    weights = jnp.exp(scores)
    attention = (weights / lax.optimization_barrier(jnp.sum(weights, axis=-1, keepdims=True))).astype(jnp.bfloat16)
    combined = multiply('bhqk,bkhe->bqhe', attention, value_rows).astype(jnp.bfloat16).reshape(batch_size, loc_count, model_width)
    hidden = inputs + multiply('bld,de->ble', combined, w_attn_out)
    normed_two = layer_norm(hidden).astype(jnp.bfloat16)
    activated = jax.nn.gelu(multiply('bld,df->blf', normed_two, w_up), approximate=True).astype(jnp.bfloat16)
    hidden = hidden + multiply('blf,fd->bld', activated, w_down)
    pooled = layer_norm(lax.optimization_barrier(jnp.mean(hidden, axis=1))).astype(jnp.bfloat16)
    logits = 2.0 * multiply('bd,dp->bp', pooled, w_value)
    raised = jnp.exp(logits)
    return raised / lax.optimization_barrier(jnp.sum(raised, axis=-1, keepdims=True))

def regret_matching(value_sums, counts):
    visits = lax.optimization_barrier(jnp.sum(counts, axis=-1, keepdims=True))
    totals = lax.optimization_barrier(jnp.sum(value_sums, axis=-1, keepdims=True))
    baseline = (totals + 1.0 / POWERS) / (visits + 1.0)
    payoff = (value_sums + baseline) / (counts + 1.0)
    regrets = jnp.zeros_like(payoff[:, 0])
    average = jnp.zeros_like(payoff[:, 0])
    for iteration in range(ITERS):
        positive = jnp.maximum(regrets, 0.0)
        policy = (positive + smoothing) / (lax.optimization_barrier(jnp.sum(positive, axis=-1, keepdims=True)) + ACTIONS * smoothing)
        current = payoff[:, iteration]
        expected = lax.optimization_barrier(jnp.sum(policy * current, axis=-1, keepdims=True))
        regrets = regrets + current - expected
        average = average + policy
    return average / ITERS

def reference(send_load, tokens, owner, joint_action, board_context, tok_embed, w_qkv, w_attn_out, w_up, w_down, w_value):
    slot_ids = jnp.arange(SLOTS, dtype=jnp.int32)
    search = slot_ids // LMAX
    slot_ranks = slot_ids % LMAX
    live_slots = slot_ranks[None, :] < jnp.take(send_load, search, axis=1)
    position = search[None, :] * P_DEV + owner // ITERS
    live_total = N_VAL * N_POS * EVAL
    chosen = jnp.nonzero(live_slots.reshape(-1), size=live_total)[0].astype(jnp.int32)
    flat_tokens = tokens.reshape(N_VAL * SLOTS, LOCS)
    flat_position = position.reshape(-1)

    def evaluate(group_ids):
        group_tokens = jnp.take(flat_tokens, group_ids, axis=0)
        group_position = jnp.take(flat_position, group_ids, axis=0)
        states = (jnp.take(tok_embed, group_tokens, axis=0).astype(jnp.float32) + jnp.take(board_context, group_position, axis=0).astype(jnp.float32)).astype(jnp.bfloat16)
        return encode(states, w_qkv, w_attn_out, w_up, w_down, w_value)
    values = lax.map(evaluate, chosen.reshape(live_total // EVAL, EVAL)).reshape(live_total, POWERS)
    state_values = jnp.zeros((N_VAL * SLOTS, POWERS), jnp.float32).at[chosen].set(values)
    cell_ids = (position * ITERS + owner % ITERS).reshape(-1)
    picked = (joint_action.reshape(-1, POWERS)[:, :, None] == jnp.arange(ACTIONS, dtype=jnp.int32)[None, None, :]).astype(jnp.float32)
    picked = picked * live_slots.reshape(-1, 1, 1).astype(jnp.float32)
    counts = jax.ops.segment_sum(picked, cell_ids, num_segments=POSITIONS * ITERS)
    value_sums = jax.ops.segment_sum(picked * state_values[:, :, None], cell_ids, num_segments=POSITIONS * ITERS)
    grid_shape = (POSITIONS, ITERS, POWERS, ACTIONS)
    avg_policy = regret_matching(value_sums.reshape(grid_shape), counts.reshape(grid_shape))
    return (state_values.reshape(N_VAL, SLOTS, POWERS), avg_policy)
```

```python
import functools
import math

import jax
import jax.numpy as jnp
from jax import lax
from jax.experimental import pallas as pl
from jax.experimental.pallas import tpu as pltpu
from jax.sharding import PartitionSpec as P

HEADS = 8
POWERS = 7
ACTIONS = 32
ITERS = 8
GROUP = 4
SMOOTHING = 0.01
F32 = jnp.float32
BF16 = jnp.bfloat16


def dot(a, b):
    return jnp.dot(a, b, preferred_element_type=F32)


def dot_nt(a, b):
    return lax.dot_general(a, b, (((1,), (1,)), ((), ())), preferred_element_type=F32)


def dot_tn(a, b):
    return lax.dot_general(a, b, (((0,), (0,)), ((), ())), preferred_element_type=F32)


def norm(u):
    centre = u - jnp.mean(u, axis=-1, keepdims=True)
    spread = jnp.mean(centre * centre, axis=-1, keepdims=True)
    return centre * lax.rsqrt(spread + 1e-05)


def span_of(load_ref, n_rows, pos, me):
    starts, total = [], jnp.int32(0)
    for v in range(n_rows):
        starts.append(total)
        total = total + load_ref[v, pos]
    low = lax.div(me * total + (n_rows - 1), jnp.int32(n_rows))
    high = lax.div((me + 1) * total + (n_rows - 1), jnp.int32(n_rows))
    return starts, low, high


def evaluate_kernel(n_rows, n_blocks, locs, *refs):
    load_ref = refs[0]
    owner_refs = refs[1 : 1 + n_blocks]
    token_refs = refs[1 + n_blocks : 1 + 2 * n_blocks]
    (
        board_ref,
        embed_ref,
        value_ref,
        qkv_hbm,
        out_hbm,
        up_hbm,
        down_hbm,
        result_ref,
        qkv_ref,
        out_ref,
        up_ref,
        down_ref,
        token_ref,
        state_ref,
        joined_ref,
        mixed_ref,
        hidden_sum,
        active_sum,
        sem,
    ) = refs[1 + 2 * n_blocks :]
    copies = [
        pltpu.make_async_copy(source, target, sem.at[i])
        for i, (source, target) in enumerate(
            (
                (qkv_hbm, qkv_ref),
                (out_hbm, out_ref),
                (up_hbm, up_ref),
                (down_hbm, down_ref),
            )
        )
    ]
    for copy in copies:
        copy.start()
    pos, me = lax.axis_index("pos"), lax.axis_index("val")
    width = embed_ref.shape[1]
    vocab = embed_ref.shape[0]
    pitch = state_ref.shape[0] // GROUP
    pad = pitch - locs
    slots = token_ref.shape[0] // n_rows
    starts, low, high = span_of(load_ref, n_rows, pos, me)
    count = high - low
    if n_blocks == 1:
        token_ref[...] = token_refs[0][...]
    else:
        for b in range(n_blocks):
            at = pl.multiple_of(lax.rem(me + b, n_rows) * slots, 8)
            token_ref[pl.ds(at, slots), :] = token_refs[b][...]
    state_ref[...] = jnp.zeros_like(state_ref)
    mixed_ref[...] = jnp.zeros_like(mixed_ref)
    head = width // HEADS
    pairs = HEADS // 2
    key_rows = 128
    lane = lax.broadcasted_iota(jnp.int32, (pitch, 2 * head), 1)
    first_half = lane < head
    key_gap = jnp.zeros((key_rows - pitch, 2 * head), F32)
    row_k = lax.broadcasted_iota(jnp.int32, (2 * key_rows, 2 * head), 0)
    lane_k = lax.broadcasted_iota(jnp.int32, (2 * key_rows, 2 * head), 1)
    ones_block = jnp.where(
        (lax.rem(row_k, key_rows) < locs) & ((row_k >= key_rows) == (lane_k >= head)), 1.0, 0.0
    ).astype(BF16)
    score_scale = head ** (-0.5) * math.log2(math.e)
    vocab_ids = lax.broadcasted_iota(jnp.int32, (vocab, locs), 0)

    def owner_at(row, slot):
        if n_blocks == 1:
            return owner_refs[0][row, slot]
        return jnp.where(row == me, owner_refs[0][0, slot], owner_refs[1][0, slot])

    copies[0].wait()
    copies[1].wait()
    copies[2].wait()

    def group_step(group, carry):
        places = []
        for g in range(GROUP):
            item = low + jnp.minimum(group * GROUP + g, count - 1)
            row, start = jnp.int32(0), jnp.int32(0)
            for v in range(1, n_rows):
                inside = item >= starts[v]
                row = jnp.where(inside, v, row)
                start = jnp.where(inside, starts[v], start)
            slot = item - start
            place = row * slots + slot
            places.append(place)
            board = lax.div(owner_at(row, slot), jnp.int32(ITERS))
            ids = token_ref[pl.ds(place, 1), :]
            hot = jnp.where(vocab_ids == ids, 1.0, 0.0).astype(BF16)
            state = dot_tn(hot, embed_ref[...]) + board_ref[board].astype(F32)
            state_ref[pl.ds(g * pitch, locs), :] = state.astype(BF16).astype(F32)
        states = state_ref[...]
        normed = norm(states).astype(BF16)
        joined_ref[...] = dot(normed, qkv_ref[...])
        for g in range(GROUP):
            rows = pl.ds(g * pitch, pitch)
            for p in range(pairs):
                at = p * 2 * head
                query = joined_ref[rows, at : at + 2 * head].astype(BF16)
                key = joined_ref[rows, width + at : width + at + 2 * head]
                value = joined_ref[rows, 2 * width + at : 2 * width + at + 2 * head] * (1.0 / 128.0)
                keys = jnp.concatenate(
                    [
                        jnp.where(first_half, key, 0.0),
                        key_gap,
                        jnp.where(first_half, 0.0, key),
                        key_gap,
                    ],
                    axis=0,
                ).astype(BF16)
                values = jnp.concatenate(
                    [
                        jnp.where(first_half, value, 0.0),
                        key_gap,
                        jnp.where(first_half, 0.0, value),
                        key_gap,
                    ],
                    axis=0,
                ).astype(BF16)
                weights = jnp.exp2(dot_nt(query, keys) * score_scale).astype(BF16)
                both = dot(weights, jnp.concatenate([values, ones_block], axis=1))
                part = both[:, : 2 * head] / both[:, 2 * head :] * 128.0
                mixed_ref[pl.ds(g * pitch, locs), at : at + 2 * head] = part[:locs]
        hidden = states + dot(mixed_ref[...].astype(BF16), out_ref[...])
        normed_two = norm(hidden).astype(BF16)
        for g in range(GROUP):
            part = hidden[g * pitch : (g + 1) * pitch]
            hidden_sum[pl.ds(places[g], 1), :] = jnp.sum(part, axis=0, keepdims=True)
        chunk = 256
        for c in range(up_ref.shape[1] // chunk):
            up = dot(normed_two, up_ref[:, c * chunk : (c + 1) * chunk])
            inner = up * (
                math.sqrt(2.0 / math.pi) + (math.sqrt(2.0 / math.pi) * 0.044715) * (up * up)
            )
            half = 0.5 * up
            active = half + half * jnp.tanh(inner)
            for g in range(GROUP):
                part = active[g * pitch : (g + 1) * pitch]
                active_sum[pl.ds(places[g], 1), c * chunk : (c + 1) * chunk] = jnp.sum(
                    part, axis=0, keepdims=True
                )
        return carry

    lax.fori_loop(0, lax.div(count + (GROUP - 1), jnp.int32(GROUP)), group_step, 0)
    copies[3].wait()
    places = result_ref.shape[0]
    place_ids = lax.broadcasted_iota(jnp.int32, (places, 1), 0)
    mine = place_ids < 0
    for v in range(n_rows):
        item = place_ids - v * slots + starts[v]
        inside = (place_ids >= v * slots) & (place_ids - v * slots < load_ref[v, pos])
        mine = mine | (inside & (item >= low) & (item < high))
    active = jnp.where(mine, active_sum[...], 0.0)
    active_high = active.astype(BF16)
    active_low = (active - active_high.astype(F32)).astype(BF16)
    final = (
        jnp.where(mine, hidden_sum[...], 0.0)
        + dot(active_high, down_ref[...])
        + dot(active_low, down_ref[...])
    )
    pooled = norm(final * (1.0 / locs)).astype(BF16)
    raised = jnp.exp(2.0 * dot(pooled, value_ref[...]))
    values = raised / jnp.sum(raised, axis=-1, keepdims=True)
    result_ref[...] = jnp.where(mine, values, 0.0)


def finish_kernel(n_rows, n_blocks, n_values, *refs):
    load_ref = refs[0]
    owner_refs = refs[1 : 1 + n_blocks]
    action_refs = refs[1 + n_blocks : 1 + 2 * n_blocks]
    value_refs = refs[1 + 2 * n_blocks : 1 + 2 * n_blocks + n_values]
    state_values_ref, policy_ref, value_ref = refs[1 + 2 * n_blocks + n_values :]
    pos, me = lax.axis_index("pos"), lax.axis_index("val")
    slots = state_values_ref.shape[0]
    boards = policy_ref.shape[0]
    total = value_refs[0][...]
    for r in value_refs[1:]:
        total = total + r[...]
    value_ref[...] = total
    state_values_ref[...] = value_ref[pl.ds(pl.multiple_of(me * slots, 8), slots), :]
    lanes = 128
    stride = boards * POWERS
    lane = lax.broadcasted_iota(jnp.int32, (slots, lanes), 1)
    lane_iter = lax.div(lane, jnp.int32(stride))
    lane_board = lax.div(lax.rem(lane, jnp.int32(stride)), jnp.int32(POWERS))
    lane_power = lax.rem(lane, jnp.int32(POWERS))
    lane_cell = jnp.where(lane < ITERS * stride, lane_board * ITERS + lane_iter, -1)
    slot_down = lax.broadcasted_iota(jnp.int32, (slots, 1), 0)
    square = lax.broadcasted_iota(jnp.int32, (slots, slots), 0) == lax.broadcasted_iota(
        jnp.int32, (slots, slots), 1
    )
    action_ids = lax.broadcasted_iota(jnp.int32, (slots, ACTIONS), 1)
    hots, rights = [], []
    for v in range(n_rows):
        if n_blocks == 1:
            row = jnp.int32(v)
            owners = owner_refs[0][v : v + 1, :]
            actions = action_refs[0][v * slots : (v + 1) * slots, :]
        else:
            row = lax.rem(me + v, n_rows)
            owners = owner_refs[v][...]
            actions = action_refs[v][...]
        values = value_ref[pl.ds(pl.multiple_of(row * slots, 8), slots), :]
        cell = jnp.sum(jnp.where(square, owners, 0), axis=1, keepdims=True)
        cell_hot = (lane_cell == cell) & (slot_down < load_ref[row, pos])
        for i in range(POWERS):
            hots.append(jnp.where(actions[:, i : i + 1] == action_ids, 1.0, 0.0))
            here = cell_hot & (lane_power == i)
            amount = jnp.where(here, values[:, i : i + 1], 0.0)
            high = amount.astype(BF16).astype(F32)
            rest = amount - high
            middle = rest.astype(BF16).astype(F32)
            rights.append(
                jnp.concatenate(
                    [jnp.where(here, 1.0, 0.0), high, middle, rest - middle], axis=1
                )
            )
    sums = dot_tn(
        jnp.concatenate(hots, axis=0).astype(BF16), jnp.concatenate(rights, axis=0).astype(BF16)
    )
    counts = sums[:, :lanes]
    value_sums = sums[:, lanes : 2 * lanes] + (
        sums[:, 2 * lanes : 3 * lanes] + sums[:, 3 * lanes :]
    )
    visits = jnp.sum(counts, axis=0, keepdims=True)
    totals = jnp.sum(value_sums, axis=0, keepdims=True)
    baseline = (totals + 1.0 / POWERS) / (visits + 1.0)
    payoff = (value_sums + baseline) / (counts + 1.0)
    regrets = jnp.zeros((ACTIONS, lanes), F32)
    average = jnp.zeros((ACTIONS, lanes), F32)
    for t in range(ITERS):
        positive = jnp.maximum(regrets, 0.0)
        policy = (positive + SMOOTHING) / (
            jnp.sum(positive, axis=0, keepdims=True) + ACTIONS * SMOOTHING
        )
        current = payoff if t == 0 else pltpu.roll(payoff, lanes - t * stride, 1)
        regrets = regrets + current - jnp.sum(policy * current, axis=0, keepdims=True)
        average = average + policy
    turned = (average / ITERS).T
    for b in range(boards):
        policy_ref[b] = turned[b * POWERS : (b + 1) * POWERS]


def local(
    send_load,
    tokens,
    owner,
    joint_action,
    board_context,
    tok_embed,
    w_qkv,
    w_attn_out,
    w_up,
    w_down,
    w_value,
):
    n_rows = lax.axis_size("val")
    slots, locs = tokens.shape[1:]
    boards = board_context.shape[0]
    width, hidden_units = w_up.shape
    tokens = tokens.reshape(slots, locs)
    joint_action = joint_action.reshape(slots, POWERS)
    if n_rows == 2:

        def rows_of(array):
            return [array, lax.ppermute(array, "val", [(0, 1), (1, 0)])]

    else:

        def rows_of(array):
            return [lax.all_gather(array, "val", axis=0, tiled=True)]

    owners, token_blocks, actions = rows_of(owner), rows_of(tokens), rows_of(joint_action)
    n_blocks = len(owners)
    vmem = pl.BlockSpec(memory_space=pltpu.VMEM)
    smem = pl.BlockSpec(memory_space=pltpu.SMEM)
    hbm = pl.BlockSpec(memory_space=pl.ANY)
    pitch = -(-locs // 8) * 8
    places = n_rows * slots
    values = pl.pallas_call(
        functools.partial(evaluate_kernel, n_rows, n_blocks, locs),
        out_shape=jax.ShapeDtypeStruct((places, POWERS), F32),
        in_specs=[smem] + [smem] * n_blocks + [vmem] * n_blocks + [vmem] * 3 + [hbm] * 4,
        out_specs=vmem,
        scratch_shapes=[
            pltpu.VMEM(w_qkv.shape, BF16),
            pltpu.VMEM(w_attn_out.shape, BF16),
            pltpu.VMEM(w_up.shape, BF16),
            pltpu.VMEM(w_down.shape, BF16),
            pltpu.VMEM((places, locs), jnp.int32),
            pltpu.VMEM((GROUP * pitch, width), F32),
            pltpu.VMEM((GROUP * pitch, 3 * width), F32),
            pltpu.VMEM((GROUP * pitch, width), F32),
            pltpu.VMEM((places, width), F32),
            pltpu.VMEM((places, hidden_units), F32),
            pltpu.SemaphoreType.DMA((4,)),
        ],
        compiler_params=pltpu.CompilerParams(vmem_limit_bytes=40 * 1024 * 1024),
        name="evaluate",
    )(
        send_load,
        *owners,
        *token_blocks,
        board_context,
        tok_embed,
        w_value,
        w_qkv,
        w_attn_out,
        w_up,
        w_down,
    )
    if n_rows == 2:
        shares = [values, lax.ppermute(values, "val", [(0, 1), (1, 0)])]
    else:
        shares = [lax.psum(values, "val")]
    state_values, policy = pl.pallas_call(
        functools.partial(finish_kernel, n_rows, n_blocks, len(shares)),
        out_shape=(
            jax.ShapeDtypeStruct((slots, POWERS), F32),
            jax.ShapeDtypeStruct((boards, POWERS, ACTIONS), F32),
        ),
        in_specs=[smem] + [vmem] * (2 * n_blocks + len(shares)),
        out_specs=(vmem, vmem),
        scratch_shapes=[pltpu.VMEM((places, POWERS), F32)],
        compiler_params=pltpu.CompilerParams(vmem_limit_bytes=40 * 1024 * 1024),
        name="finish",
    )(send_load, *owners, *actions, *shares)
    return (state_values[None], policy)


def solution(mesh):
    in_specs = (
        P(),
        P("val", "pos", None),
        P("val", "pos"),
        P("val", "pos", None),
        P("pos", None, None),
        P(),
        P(),
        P(),
        P(),
        P(),
        P(),
    )
    out_specs = (P("val", "pos", None), P("pos", None, None))
    return jax.shard_map(local, mesh=mesh, in_specs=in_specs, out_specs=out_specs, check_vma=False)
```

```python
import functools
import math

import jax
import jax.numpy as jnp
from jax import lax
from jax.experimental import pallas as pl
from jax.experimental.pallas import tpu as pltpu
from jax.sharding import PartitionSpec as P

HEADS = 8
POWERS = 7
ACTIONS = 32
ITERS = 8
PARTS = 1
SIZE = 5
SKEW = True
LANES = 128
SMOOTHING = 0.01
F32 = jnp.float32
BF16 = jnp.bfloat16


def dot(a, b):
    return jnp.dot(a, b, preferred_element_type=F32)


def dot_nt(a, b):
    return lax.dot_general(a, b, (((1,), (1,)), ((), ())), preferred_element_type=F32)


def dot_tn(a, b):
    return lax.dot_general(a, b, (((0,), (0,)), ((), ())), preferred_element_type=F32)


def norm(u):
    centre = u - jnp.mean(u, axis=-1, keepdims=True)
    spread = jnp.mean(centre * centre, axis=-1, keepdims=True)
    return centre * lax.rsqrt(spread + 1e-05)


def evaluate_kernel(n_rows, n_blocks, locs, *refs):
    load_ref = refs[0]
    owner_refs = refs[1 : 1 + n_blocks]
    token_refs = refs[1 + n_blocks : 1 + 2 * n_blocks]
    (
        board_ref,
        embed_ref,
        value_ref,
        qkv_ref,
        out_ref,
        up_ref,
        down_ref,
    ) = refs[1 + 3 * n_blocks : 8 + 3 * n_blocks]
    result_ref, token_ref, hidden_sum, active_sum = refs[8 + 3 * n_blocks : 12 + 3 * n_blocks]
    scratch = refs[12 + 3 * n_blocks :]
    parts = [scratch[3 * k : 3 * k + 3] for k in range(PARTS)]
    pos, me = lax.axis_index("pos"), lax.axis_index("val")
    vocab, width = embed_ref.shape
    pitch = parts[0][0].shape[0] // SIZE
    places = token_ref.shape[0]
    slots = places // n_rows
    starts, total = [], jnp.int32(0)
    for v in range(n_rows):
        starts.append(total)
        total = total + load_ref[v, pos]
    low = lax.div(me * total + (n_rows - 1), jnp.int32(n_rows))
    high = lax.div((me + 1) * total + (n_rows - 1), jnp.int32(n_rows))
    count = high - low

    def block_of(row):
        return lax.rem(row - me + n_rows, n_rows) if n_blocks == 2 else row

    def owner_at(block, slot):
        if n_blocks == 1:
            return owner_refs[0][block, slot]
        return jnp.where(block == 0, owner_refs[0][0, slot], owner_refs[1][0, slot])

    for b in range(n_blocks):
        part = places // n_blocks
        token_ref[b * part : (b + 1) * part, :] = token_refs[b][...]
    for state_ref, _, mixed_ref in parts:
        state_ref[...] = jnp.zeros_like(state_ref)
        mixed_ref[...] = jnp.zeros_like(mixed_ref)
    hidden_sum[...] = jnp.zeros_like(hidden_sum)
    active_sum[...] = jnp.zeros_like(active_sum)
    head = width // HEADS
    pair = 2 * head
    key_gap = jnp.zeros((LANES - pitch, pair), BF16)
    head_gap = jnp.zeros((head, LANES), BF16)
    first_half = lax.broadcasted_iota(jnp.int32, (pitch, pair), 1) < head
    first_scale = jnp.where(first_half, 1.0 / 128.0, 0.0).astype(BF16)
    second_scale = jnp.where(first_half, 0.0, 1.0 / 128.0).astype(BF16)
    row_k = lax.broadcasted_iota(jnp.int32, (2 * LANES, pair), 0)
    lane_k = lax.broadcasted_iota(jnp.int32, (2 * LANES, pair), 1)
    ones_block = jnp.where(
        (lax.rem(row_k, jnp.int32(LANES)) < locs) & ((row_k >= LANES) == (lane_k >= head)), 1.0, 0.0
    ).astype(BF16)
    score_scale = head ** (-0.5) * math.log2(math.e)
    vocab_ids = lax.broadcasted_iota(jnp.int32, (vocab, locs), 0)

    def embed_part(first, state_ref):
        at = []
        for g in range(SIZE):
            item = low + jnp.minimum(first + g, count - 1)
            row, start = jnp.int32(0), jnp.int32(0)
            for v in range(1, n_rows):
                inside = item >= starts[v]
                row = jnp.where(inside, v, row)
                start = jnp.where(inside, starts[v], start)
            slot = item - start
            block = block_of(row)
            place = block * slots + slot
            at.append(place)
            board = lax.div(owner_at(block, slot), jnp.int32(ITERS))
            ids = token_ref[pl.ds(place, 1), :]
            hot = jnp.where(vocab_ids == ids, 1.0, 0.0).astype(BF16)
            state = dot_tn(hot, embed_ref[...]) + board_ref[board]
            state_ref[g * pitch : g * pitch + locs, :] = state.astype(BF16).astype(F32)
        return at

    def join_part(state_ref, joined_ref):
        normed = norm(state_ref[...]).astype(BF16)
        joined_ref[...] = dot(normed, qkv_ref[...]).astype(BF16)

    def attend_part(joined_ref, mixed_ref):
        for g in range(SIZE):
            rows = slice(g * pitch, (g + 1) * pitch)
            for p in range(HEADS // 2):
                lane = p * pair
                query = joined_ref[rows, lane : lane + pair]
                key = joined_ref[rows, width + lane : width + lane + pair]
                value = joined_ref[rows, 2 * width + lane : 2 * width + lane + pair]
                turned = jnp.concatenate([key, key_gap], axis=0).T
                keys = jnp.concatenate(
                    [
                        jnp.concatenate([turned[:head], head_gap], axis=0),
                        jnp.concatenate([head_gap, turned[head:]], axis=0),
                    ],
                    axis=1,
                )
                values = jnp.concatenate(
                    [value * first_scale, key_gap, value * second_scale, key_gap], axis=0
                )
                weights = jnp.exp2(dot(query, keys) * score_scale).astype(BF16)
                both = dot(weights, jnp.concatenate([values, ones_block], axis=1))
                part = (both[:, :pair] / both[:, pair:] * 128.0).astype(BF16)
                mixed_ref[g * pitch : g * pitch + locs, lane : lane + pair] = part[:locs]

    def hide_part(state_ref, mixed_ref, at):
        hidden = state_ref[...] + dot(mixed_ref[...], out_ref[...])
        for g in range(SIZE):
            part = hidden[g * pitch : (g + 1) * pitch]
            hidden_sum[pl.ds(at[g], 1), :] = jnp.sum(part, axis=0, keepdims=True)
        return norm(hidden).astype(BF16)

    def feed_part(normed_two, at):
        chunk = 256
        for c in range(up_ref.shape[1] // chunk):
            up = dot(normed_two, up_ref[:, c * chunk : (c + 1) * chunk])
            inner = up * (
                math.sqrt(2.0 / math.pi) + (math.sqrt(2.0 / math.pi) * 0.044715) * (up * up)
            )
            half = 0.5 * up
            active = half + half * jnp.tanh(inner)
            for g in range(SIZE):
                part = active[g * pitch : (g + 1) * pitch]
                active_sum[pl.ds(at[g], 1), c * chunk : (c + 1) * chunk] = jnp.sum(
                    part, axis=0, keepdims=True
                )

    def group_step(group, carry):
        at, normed_two = {}, {}
        for stage in range(PARTS + 4):
            for k in range(PARTS):
                state_ref, joined_ref, mixed_ref = parts[k]
                turn = stage - (k if SKEW else 0)
                if turn == 0:
                    at[k] = embed_part((group * PARTS + k) * SIZE, state_ref)
                elif turn == 1:
                    join_part(state_ref, joined_ref)
                elif turn == 2:
                    attend_part(joined_ref, mixed_ref)
                elif turn == 3:
                    normed_two[k] = hide_part(state_ref, mixed_ref, at[k])
                elif turn == 4:
                    feed_part(normed_two[k], at[k])
        return carry

    whole = PARTS * SIZE
    lax.fori_loop(0, lax.div(count + (whole - 1), jnp.int32(whole)), group_step, 0)
    active = active_sum[...]
    active_high = active.astype(BF16)
    active_low = (active - active_high.astype(F32)).astype(BF16)
    lowered = dot(jnp.concatenate([active_high, active_low], axis=0), down_ref[...])
    final = hidden_sum[...] + (lowered[:places] + lowered[places:])
    pooled = norm(final * (1.0 / locs)).astype(BF16)
    raised = jnp.exp(2.0 * dot_nt(value_ref[...], pooled))
    values = raised / jnp.sum(raised, axis=0, keepdims=True)
    lane = lax.broadcasted_iota(jnp.int32, (POWERS, places), 1)
    mine = lane < 0
    for v in range(n_rows):
        slot = lane - block_of(v) * slots
        item = slot + starts[v]
        mine = mine | (
            (slot >= 0) & (slot < load_ref[v, pos]) & (item >= low) & (item < high)
        )
    result_ref[...] = jnp.where(mine, values, 0.0)


def fetch_kernel(n, *refs):
    board_ref, sources = refs[0], refs[1 : 1 + n]
    boards_ref, targets, sem = refs[1 + n], refs[2 + n : 2 + 2 * n], refs[2 + 2 * n]
    copies = [
        pltpu.make_async_copy(source, target, sem.at[i])
        for i, (source, target) in enumerate(zip(sources, targets))
    ]
    for copy in copies:
        copy.start()
    board = board_ref[...].astype(F32)
    for b in range(boards_ref.shape[0]):
        boards_ref[b] = board[:, b, :]
    for copy in copies:
        copy.wait()


def finish_kernel(n_rows, n_blocks, *refs):
    load_ref = refs[0]
    owner_refs = refs[1 : 1 + n_blocks]
    action_refs = refs[1 + n_blocks : 1 + 2 * n_blocks]
    value_refs = refs[1 + 2 * n_blocks : 1 + 3 * n_blocks]
    state_values_ref, policy_ref, action_ref, value_ref = refs[1 + 3 * n_blocks :]
    pos, me = lax.axis_index("pos"), lax.axis_index("val")
    slots = state_values_ref.shape[2]
    boards = policy_ref.shape[1]
    places = value_ref.shape[0]
    pad = 8
    lane = lax.broadcasted_iota(jnp.int32, (slots, LANES), 1)
    lane_cell = lax.div(lane, jnp.int32(pad))
    slot_down = lax.broadcasted_iota(jnp.int32, (slots, 1), 0)
    square = lax.broadcasted_iota(jnp.int32, (slots, slots), 0) == lax.broadcasted_iota(
        jnp.int32, (slots, slots), 1
    )
    for v in range(n_rows):
        if n_blocks == 1:
            row = jnp.int32(v)
            owners = owner_refs[0][v : v + 1, :]
            actions = [action_refs[0][i, v : v + 1, :] for i in range(POWERS)]
            values = value_refs[0][:, v * slots : (v + 1) * slots]
        else:
            row = lax.rem(me + v, n_rows)
            owners = owner_refs[v][...]
            actions = [action_refs[v][i] for i in range(POWERS)]
            here, there = v * slots, (1 - v) * slots
            values = (
                value_refs[0][:, here : here + slots] + value_refs[1][:, there : there + slots]
            )

        def store(values=values):
            for i in range(POWERS):
                state_values_ref[i] = values[i : i + 1]

        if n_blocks == 1:
            pl.when(me == v)(store)
        elif v == 0:
            store()
        blank = jnp.zeros((1, slots), F32)
        stacked = jnp.concatenate(
            [values, blank] + [a.astype(F32) for a in actions] + [blank], axis=0
        )
        turned = stacked.T
        cell = jnp.sum(jnp.where(square, owners, 0), axis=1, keepdims=True)
        spread = jnp.concatenate([turned[:, :pad]] * (LANES // pad), axis=1)
        chosen = jnp.concatenate([turned[:, pad:]] * (LANES // pad), axis=1).astype(jnp.int32)
        live = (lane_cell == cell) & (slot_down < load_ref[row, pos])
        action_ref[v * slots : (v + 1) * slots, :] = jnp.where(live, chosen, -1)
        value_ref[v * slots : (v + 1) * slots, :] = spread
    action_ids = lax.broadcasted_iota(jnp.int32, (ACTIONS, LANES), 0)
    unit = 16

    def add_slots(step, sums):
        counts, value_sums = sums
        base = step * unit
        for k in range(unit):
            hit = action_ids == action_ref[pl.ds(base + k, 1), :]
            counts = counts + jnp.where(hit, 1.0, 0.0)
            value_sums = value_sums + jnp.where(hit, value_ref[pl.ds(base + k, 1), :], 0.0)
        return counts, value_sums

    sums = (jnp.zeros((ACTIONS, LANES), F32), jnp.zeros((ACTIONS, LANES), F32))
    if places <= 2 * unit:
        for step in range(places // unit):
            sums = add_slots(step, sums)
    else:
        sums = lax.fori_loop(0, places // unit, add_slots, sums)
    counts, value_sums = sums
    visits = jnp.sum(counts, axis=0, keepdims=True)
    totals = jnp.sum(value_sums, axis=0, keepdims=True)
    baseline = (totals + 1.0 / POWERS) / (visits + 1.0)
    payoff = (value_sums + baseline) / (counts + 1.0)
    regrets = jnp.zeros((ACTIONS, LANES), F32)
    average = jnp.zeros((ACTIONS, LANES), F32)
    for t in range(ITERS):
        positive = jnp.maximum(regrets, 0.0)
        policy = (positive + SMOOTHING) / (
            jnp.sum(positive, axis=0, keepdims=True) + ACTIONS * SMOOTHING
        )
        current = payoff if t == 0 else pltpu.roll(payoff, LANES - t * pad, 1)
        regrets = regrets + current - jnp.sum(policy * current, axis=0, keepdims=True)
        average = average + policy
    turned = (average / ITERS).T
    for b in range(boards):
        first = b * ITERS * pad
        policy_ref[:, b, :] = turned[first : first + POWERS]


def local(
    send_load,
    tokens,
    owner,
    joint_action,
    board_context,
    tok_embed,
    w_qkv,
    w_attn_out,
    w_up,
    w_down,
    w_value,
):
    n_rows = lax.axis_size("val")
    slots, locs = tokens.shape[1:]
    boards = board_context.shape[0]
    width, hidden_units = w_up.shape
    tokens = tokens.reshape(slots, locs)
    actions = jnp.transpose(joint_action, (2, 0, 1))
    if n_rows == 2:

        def rows_of(array, axis):
            return [array, lax.ppermute(array, "val", [(0, 1), (1, 0)])]

    else:

        def rows_of(array, axis):
            return [lax.all_gather(array, "val", axis=axis, tiled=True)]

    token_blocks, owners, actions = rows_of(tokens, 0), rows_of(owner, 0), rows_of(actions, 1)
    n_blocks = len(owners)
    vmem = pl.BlockSpec(memory_space=pltpu.VMEM)
    smem = pl.BlockSpec(memory_space=pltpu.SMEM)
    hbm = pl.BlockSpec(memory_space=pl.ANY)
    pitch = -(-locs // 16) * 16
    places = n_rows * slots
    weights = (tok_embed, w_qkv, w_attn_out, w_up, w_down)
    held = pl.pallas_call(
        functools.partial(fetch_kernel, len(weights)),
        out_shape=[pltpu.VMEM((boards, locs, width), F32)]
        + [pltpu.VMEM(w.shape, BF16) for w in weights],
        in_specs=[vmem] + [hbm] * len(weights),
        out_specs=[vmem] * (1 + len(weights)),
        scratch_shapes=[pltpu.SemaphoreType.DMA((len(weights),))],
        compiler_params=pltpu.CompilerParams(vmem_limit_bytes=58 * 1024 * 1024),
        cost_estimate=pl.CostEstimate(flops=0, bytes_accessed=9000000, transcendentals=0),
        name="fetch",
    )(jnp.transpose(board_context, (1, 0, 2)), *weights)
    values = pl.pallas_call(
        functools.partial(evaluate_kernel, n_rows, n_blocks, locs),
        out_shape=jax.ShapeDtypeStruct((POWERS, places), F32),
        in_specs=[smem] + [smem] * n_blocks + [vmem] * (2 * n_blocks + 7),
        out_specs=vmem,
        scratch_shapes=[
            pltpu.VMEM((places, locs), jnp.int32),
            pltpu.VMEM((places, width), F32),
            pltpu.VMEM((places, hidden_units), F32),
        ]
        + [
            pltpu.VMEM((SIZE * pitch, width), F32),
            pltpu.VMEM((SIZE * pitch, 3 * width), BF16),
            pltpu.VMEM((SIZE * pitch, width), BF16),
        ]
        * PARTS,
        compiler_params=pltpu.CompilerParams(vmem_limit_bytes=28 * 1024 * 1024),
        name="evaluate",
    )(send_load, *owners, *token_blocks, *actions, *held[:2], w_value.T, *held[2:])
    if n_rows == 2:
        shares = [values, lax.ppermute(values, "val", [(0, 1), (1, 0)])]
    else:
        shares = [lax.psum(values, "val")]
    state_values, policy = pl.pallas_call(
        functools.partial(finish_kernel, n_rows, n_blocks),
        out_shape=(
            jax.ShapeDtypeStruct((POWERS, 1, slots), F32),
            jax.ShapeDtypeStruct((POWERS, boards, ACTIONS), F32),
        ),
        in_specs=[smem] + [vmem] * (3 * n_blocks),
        out_specs=(vmem, vmem),
        scratch_shapes=[
            pltpu.VMEM((places, LANES), jnp.int32),
            pltpu.VMEM((places, LANES), F32),
        ],
        compiler_params=pltpu.CompilerParams(vmem_limit_bytes=16 * 1024 * 1024),
        name="finish",
    )(send_load, *owners, *actions, *shares)
    return (jnp.transpose(state_values, (1, 2, 0)), jnp.transpose(policy, (1, 0, 2)))


def solution(mesh):
    in_specs = (
        P(),
        P("val", "pos", None),
        P("val", "pos"),
        P("val", "pos", None),
        P("pos", None, None),
        P(),
        P(),
        P(),
        P(),
        P(),
        P(),
    )
    out_specs = (P("val", "pos", None), P("pos", None, None))
    return jax.shard_map(local, mesh=mesh, in_specs=in_specs, out_specs=out_specs, check_vma=False)
```

```python
import functools
import math

import jax
import jax.numpy as jnp
from jax import lax
from jax.experimental import pallas as pl
from jax.experimental.pallas import tpu as pltpu
from jax.sharding import PartitionSpec as P

HEADS = 8
POWERS = 7
ACTIONS = 32
ITERS = 8
SIZES = (5, 6)
LANES = 128
SMOOTHING = 0.01
F32 = jnp.float32
BF16 = jnp.bfloat16


def dot(a, b):
    return jnp.dot(a, b, preferred_element_type=F32)


def dot_nt(a, b):
    return lax.dot_general(a, b, (((1,), (1,)), ((), ())), preferred_element_type=F32)


def dot_tn(a, b):
    return lax.dot_general(a, b, (((0,), (0,)), ((), ())), preferred_element_type=F32)


def norm(u):
    centre = u - jnp.mean(u, axis=-1, keepdims=True)
    spread = jnp.mean(centre * centre, axis=-1, keepdims=True)
    return centre * lax.rsqrt(spread + 1e-05)


def evaluate_kernel(n_rows, n_blocks, locs, *refs):
    load_ref = refs[0]
    owner_refs = refs[1 : 1 + n_blocks]
    token_refs = refs[1 + n_blocks : 1 + 2 * n_blocks]
    (
        board_ref,
        embed_ref,
        value_ref,
        qkv_ref,
        out_ref,
        up_ref,
        down_ref,
    ) = refs[1 + 3 * n_blocks : 8 + 3 * n_blocks]
    result_ref, token_ref, sum_ref = refs[8 + 3 * n_blocks : 11 + 3 * n_blocks]
    scratch = refs[11 + 3 * n_blocks :]
    pos, me = lax.axis_index("pos"), lax.axis_index("val")
    vocab, width = embed_ref.shape
    pitch = -(-locs // 16) * 16
    places = token_ref.shape[0]
    slots = places // n_rows
    starts, total = [], jnp.int32(0)
    for v in range(n_rows):
        starts.append(total)
        total = total + load_ref[v, pos]
    low = lax.div(me * total + (n_rows - 1), jnp.int32(n_rows))
    high = lax.div((me + 1) * total + (n_rows - 1), jnp.int32(n_rows))
    count = high - low

    def block_of(row):
        return lax.rem(row - me + n_rows, n_rows) if n_blocks == 2 else row

    def owner_at(block, slot):
        if n_blocks == 1:
            return owner_refs[0][block, slot]
        return jnp.where(block == 0, owner_refs[0][0, slot], owner_refs[1][0, slot])

    for b in range(n_blocks):
        part = places // n_blocks
        token_ref[b * part : (b + 1) * part, :] = token_refs[b][...]
    sum_ref[...] = jnp.zeros_like(sum_ref)
    for r in (scratch[0], scratch[1], scratch[3]):
        r[...] = jnp.zeros_like(r)
    head = width // HEADS
    pair = 2 * head
    key_gap = jnp.zeros((LANES - pitch, pair), BF16)
    head_gap = jnp.zeros((head, LANES), BF16)
    first_half = lax.broadcasted_iota(jnp.int32, (pitch, pair), 1) < head
    first_scale = jnp.where(first_half, 1.0 / 128.0, 0.0).astype(BF16)
    second_scale = jnp.where(first_half, 0.0, 1.0 / 128.0).astype(BF16)
    row_k = lax.broadcasted_iota(jnp.int32, (2 * LANES, pair), 0)
    lane_k = lax.broadcasted_iota(jnp.int32, (2 * LANES, pair), 1)
    ones_block = jnp.where(
        (lax.rem(row_k, jnp.int32(LANES)) < locs) & ((row_k >= LANES) == (lane_k >= head)), 1.0, 0.0
    ).astype(BF16)
    score_scale = head ** (-0.5) * math.log2(math.e)
    selector_row = lax.broadcasted_iota(jnp.int32, (16, max(SIZES) * pitch), 0)
    selector_lane = lax.broadcasted_iota(jnp.int32, (16, max(SIZES) * pitch), 1)
    vocab_ids = lax.broadcasted_iota(jnp.int32, (vocab, locs), 0)

    def group_step(size, group, carry):
        first = group * size
        state_ref, exact_ref, joined_ref, mixed_ref, normed_ref, hidden_ref = scratch
        rows = slice(0, size * pitch)
        at = []
        selector = jnp.where(
            (lax.div(selector_lane, jnp.int32(pitch)) == selector_row)
            & (lax.rem(selector_lane, jnp.int32(pitch)) < locs),
            1.0,
            0.0,
        ).astype(BF16)[:, rows]

        def embed(g):
            item = low + jnp.minimum(first + g, count - 1)
            row, start = jnp.int32(0), jnp.int32(0)
            for v in range(1, n_rows):
                inside = item >= starts[v]
                row = jnp.where(inside, v, row)
                start = jnp.where(inside, starts[v], start)
            slot = item - start
            block = block_of(row)
            place = block * slots + slot
            at.append(place)
            board = lax.div(owner_at(block, slot), jnp.int32(ITERS))
            ids = token_ref[pl.ds(place, 1), :]
            hot = jnp.where(vocab_ids == ids, 1.0, 0.0).astype(BF16)
            exact = (dot_tn(hot, embed_ref[...]) + board_ref[board]).astype(BF16)
            exact_ref[g * pitch : g * pitch + locs, :] = exact
            state_ref[g * pitch : g * pitch + locs, :] = exact.astype(F32)

        def add_sums(lane, array):
            sums = dot(selector, array)
            for g in range(size):
                sum_ref[pl.ds(at[g], 1), lane : lane + sums.shape[1]] = sums[g : g + 1]

        def norm_state(g):
            here = slice(g * pitch, (g + 1) * pitch)
            normed_ref[here] = norm(state_ref[here]).astype(BF16)

        def join():
            joined_ref[rows] = dot(normed_ref[rows], qkv_ref[...]).astype(BF16)

        def attend(g, p):
            here = slice(g * pitch, (g + 1) * pitch)
            lane = p * pair
            query = joined_ref[here, lane : lane + pair]
            key = joined_ref[here, width + lane : width + lane + pair]
            value = joined_ref[here, 2 * width + lane : 2 * width + lane + pair]
            turned = jnp.concatenate([key, key_gap], axis=0).T
            keys = jnp.concatenate(
                [
                    jnp.concatenate([turned[:head], head_gap], axis=0),
                    jnp.concatenate([head_gap, turned[head:]], axis=0),
                ],
                axis=1,
            )
            values = jnp.concatenate(
                [value * first_scale, key_gap, value * second_scale, key_gap], axis=0
            )
            weights = jnp.exp2(dot(query, keys) * score_scale).astype(BF16)
            both = dot(weights, jnp.concatenate([values, ones_block], axis=1))
            part = (both[:, :pair] / both[:, pair:] * 128.0).astype(BF16)
            mixed_ref[here, lane : lane + pair] = part

        def hide():
            hidden_ref[rows] = state_ref[rows] + dot(mixed_ref[rows], out_ref[...])

        def norm_hidden(g):
            here = slice(g * pitch, (g + 1) * pitch)
            normed_ref[here] = norm(hidden_ref[here]).astype(BF16)

        def feed():
            up = dot(normed_ref[rows], up_ref[...]).astype(BF16)
            inner = up * (
                jnp.asarray(math.sqrt(2.0 / math.pi), BF16)
                + jnp.asarray(math.sqrt(2.0 / math.pi) * 0.044715, BF16) * (up * up)
            )
            half = jnp.asarray(0.5, BF16) * up
            add_sums(2 * width, half + half * jnp.tanh(inner))

        for g in range(size):
            embed(g)
        for g in range(size):
            norm_state(g)
        join()
        for g in range(size):
            for p in range(HEADS // 2):
                attend(g, p)
        hide()
        for g in range(size):
            norm_hidden(g)
        add_sums(0, exact_ref[rows])
        add_sums(width, mixed_ref[rows])
        feed()
        return carry

    small, large = SIZES
    steps = lax.div(count + (large - 1), jnp.int32(large))
    fits = steps * small >= count
    for size, chosen in ((small, fits), (large, jnp.logical_not(fits))):
        lax.fori_loop(0, jnp.where(chosen, steps, 0), functools.partial(group_step, size), 0)
    mixed_active = sum_ref[:, width:]
    upper = mixed_active.astype(BF16)
    halves = jnp.concatenate([upper, (mixed_active - upper.astype(F32)).astype(BF16)], axis=0)
    added = dot(halves[:, :width], out_ref[...]) + dot(halves[:, width:], down_ref[...])
    final = sum_ref[:, :width] + (added[:places] + added[places:])
    pooled = norm(final * (1.0 / locs)).astype(BF16)
    raised = jnp.exp(2.0 * dot_nt(value_ref[...], pooled))
    values = raised / jnp.sum(raised, axis=0, keepdims=True)
    lane = lax.broadcasted_iota(jnp.int32, (POWERS, places), 1)
    mine = lane < 0
    for v in range(n_rows):
        slot = lane - block_of(v) * slots
        item = slot + starts[v]
        mine = mine | (
            (slot >= 0) & (slot < load_ref[v, pos]) & (item >= low) & (item < high)
        )
    result_ref[...] = jnp.where(mine, values, 0.0)


def fetch_kernel(n, *refs):
    sources = refs[:n]
    boards_ref, targets = refs[n], refs[n + 1 : 2 * n]
    board_ref, sem = refs[2 * n :]
    copies = [
        pltpu.make_async_copy(source, target, sem.at[i])
        for i, (source, target) in enumerate(zip(sources, (board_ref,) + targets))
    ]
    for copy in copies:
        copy.start()
    copies[0].wait()
    board = board_ref[...].astype(F32)
    for b in range(boards_ref.shape[0]):
        boards_ref[b] = board[:, b, :]
    for copy in copies[1:]:
        copy.wait()


def finish_kernel(n_rows, n_blocks, *refs):
    load_ref = refs[0]
    owner_refs = refs[1 : 1 + n_blocks]
    action_refs = refs[1 + n_blocks : 1 + 2 * n_blocks]
    value_refs = refs[1 + 2 * n_blocks : 1 + 3 * n_blocks]
    state_values_ref, policy_ref, action_ref, value_ref = refs[1 + 3 * n_blocks :]
    pos, me = lax.axis_index("pos"), lax.axis_index("val")
    slots = state_values_ref.shape[2]
    boards = policy_ref.shape[1]
    places = value_ref.shape[0]
    pad = 8
    lane = lax.broadcasted_iota(jnp.int32, (slots, LANES), 1)
    lane_cell = lax.div(lane, jnp.int32(pad))
    slot_down = lax.broadcasted_iota(jnp.int32, (slots, 1), 0)
    square = lax.broadcasted_iota(jnp.int32, (slots, slots), 0) == lax.broadcasted_iota(
        jnp.int32, (slots, slots), 1
    )
    for v in range(n_rows):
        if n_blocks == 1:
            row = jnp.int32(v)
            owners = owner_refs[0][v : v + 1, :]
            actions = [action_refs[0][i, v : v + 1, :] for i in range(POWERS)]
            values = value_refs[0][:, v * slots : (v + 1) * slots]
        else:
            row = lax.rem(me + v, n_rows)
            owners = owner_refs[v][...]
            actions = [action_refs[v][i] for i in range(POWERS)]
            here, there = v * slots, (1 - v) * slots
            values = (
                value_refs[0][:, here : here + slots] + value_refs[1][:, there : there + slots]
            )

        def store(values=values):
            for i in range(POWERS):
                state_values_ref[i] = values[i : i + 1]

        if n_blocks == 1:
            pl.when(me == v)(store)
        elif v == 0:
            store()
        blank = jnp.zeros((1, slots), F32)
        stacked = jnp.concatenate(
            [values, blank] + [a.astype(F32) for a in actions] + [blank], axis=0
        )
        turned = stacked.T
        cell = jnp.sum(jnp.where(square, owners, 0), axis=1, keepdims=True)
        spread = jnp.concatenate([turned[:, :pad]] * (LANES // pad), axis=1)
        chosen = jnp.concatenate([turned[:, pad:]] * (LANES // pad), axis=1).astype(jnp.int32)
        live = (lane_cell == cell) & (slot_down < load_ref[row, pos])
        action_ref[v * slots : (v + 1) * slots, :] = jnp.where(live, chosen, -1)
        value_ref[v * slots : (v + 1) * slots, :] = spread
    action_ids = lax.broadcasted_iota(jnp.int32, (ACTIONS, LANES), 0)
    unit = 16

    def add_slots(step, sums):
        counts, value_sums = sums
        base = step * unit
        for k in range(unit):
            hit = action_ids == action_ref[pl.ds(base + k, 1), :]
            counts = counts + jnp.where(hit, 1.0, 0.0)
            value_sums = value_sums + jnp.where(hit, value_ref[pl.ds(base + k, 1), :], 0.0)
        return counts, value_sums

    sums = (jnp.zeros((ACTIONS, LANES), F32), jnp.zeros((ACTIONS, LANES), F32))
    if places <= 2 * unit:
        for step in range(places // unit):
            sums = add_slots(step, sums)
    else:
        sums = lax.fori_loop(0, places // unit, add_slots, sums)
    counts, value_sums = sums
    visits = jnp.sum(counts, axis=0, keepdims=True)
    totals = jnp.sum(value_sums, axis=0, keepdims=True)
    baseline = (totals + 1.0 / POWERS) / (visits + 1.0)
    payoff = (value_sums + baseline) / (counts + 1.0)
    regrets = jnp.zeros((ACTIONS, LANES), F32)
    average = jnp.zeros((ACTIONS, LANES), F32)
    for t in range(ITERS):
        positive = jnp.maximum(regrets, 0.0)
        policy = (positive + SMOOTHING) / (
            jnp.sum(positive, axis=0, keepdims=True) + ACTIONS * SMOOTHING
        )
        current = payoff if t == 0 else pltpu.roll(payoff, LANES - t * pad, 1)
        regrets = regrets + current - jnp.sum(policy * current, axis=0, keepdims=True)
        average = average + policy
    turned = (average / ITERS).T
    for b in range(boards):
        first = b * ITERS * pad
        policy_ref[:, b, :] = turned[first : first + POWERS]


def local(
    send_load,
    tokens,
    owner,
    joint_action,
    board_context,
    tok_embed,
    w_qkv,
    w_attn_out,
    w_up,
    w_down,
    w_value,
):
    n_rows = lax.axis_size("val")
    slots, locs = tokens.shape[1:]
    boards = board_context.shape[0]
    width, hidden_units = w_up.shape
    tokens = tokens.reshape(slots, locs)
    actions = jnp.transpose(joint_action, (2, 0, 1))
    if n_rows == 2:

        def rows_of(array, axis):
            return [array, lax.ppermute(array, "val", [(0, 1), (1, 0)])]

    else:

        def rows_of(array, axis):
            return [lax.all_gather(array, "val", axis=axis, tiled=True)]

    token_blocks, owners, actions = rows_of(tokens, 0), rows_of(owner, 0), rows_of(actions, 1)
    n_blocks = len(owners)
    vmem = pl.BlockSpec(memory_space=pltpu.VMEM)
    smem = pl.BlockSpec(memory_space=pltpu.SMEM)
    hbm = pl.BlockSpec(memory_space=pl.ANY)
    rows = max(SIZES) * (-(-locs // 16) * 16)
    places = n_rows * slots
    inputs = (jnp.transpose(board_context, (1, 0, 2)), tok_embed, w_qkv, w_attn_out, w_up, w_down)
    held = pl.pallas_call(
        functools.partial(fetch_kernel, len(inputs)),
        out_shape=[pltpu.VMEM((boards, locs, width), F32)]
        + [pltpu.VMEM(w.shape, BF16) for w in inputs[1:]],
        in_specs=[hbm] * len(inputs),
        out_specs=[vmem] * len(inputs),
        scratch_shapes=[
            pltpu.VMEM(inputs[0].shape, BF16),
            pltpu.SemaphoreType.DMA((len(inputs),)),
        ],
        compiler_params=pltpu.CompilerParams(vmem_limit_bytes=58 * 1024 * 1024),
        cost_estimate=pl.CostEstimate(flops=0, bytes_accessed=9000000, transcendentals=0),
        name="fetch",
    )(*inputs)
    values = pl.pallas_call(
        functools.partial(evaluate_kernel, n_rows, n_blocks, locs),
        out_shape=jax.ShapeDtypeStruct((POWERS, places), F32),
        in_specs=[smem] + [smem] * n_blocks + [vmem] * (2 * n_blocks + 7),
        out_specs=vmem,
        scratch_shapes=[
            pltpu.VMEM((places, locs), jnp.int32),
            pltpu.VMEM((places, 2 * width + hidden_units), F32),
        ]
        + [
            pltpu.VMEM((rows, width), F32),
            pltpu.VMEM((rows, width), BF16),
            pltpu.VMEM((rows, 3 * width), BF16),
            pltpu.VMEM((rows, width), BF16),
            pltpu.VMEM((rows, width), BF16),
            pltpu.VMEM((rows, width), F32),
        ],
        compiler_params=pltpu.CompilerParams(vmem_limit_bytes=28 * 1024 * 1024),
        name="evaluate",
    )(send_load, *owners, *token_blocks, *actions, *held[:2], w_value.T, *held[2:])
    if n_rows == 2:
        shares = [values, lax.ppermute(values, "val", [(0, 1), (1, 0)])]
    else:
        shares = [lax.psum(values, "val")]
    state_values, policy = pl.pallas_call(
        functools.partial(finish_kernel, n_rows, n_blocks),
        out_shape=(
            jax.ShapeDtypeStruct((POWERS, 1, slots), F32),
            jax.ShapeDtypeStruct((POWERS, boards, ACTIONS), F32),
        ),
        in_specs=[smem] + [vmem] * (3 * n_blocks),
        out_specs=(vmem, vmem),
        scratch_shapes=[
            pltpu.VMEM((places, LANES), jnp.int32),
            pltpu.VMEM((places, LANES), F32),
        ],
        compiler_params=pltpu.CompilerParams(vmem_limit_bytes=16 * 1024 * 1024),
        name="finish",
    )(send_load, *owners, *actions, *shares)
    return (jnp.transpose(state_values, (1, 2, 0)), jnp.transpose(policy, (1, 0, 2)))


def solution(mesh):
    in_specs = (
        P(),
        P("val", "pos", None),
        P("val", "pos"),
        P("val", "pos", None),
        P("pos", None, None),
        P(),
        P(),
        P(),
        P(),
        P(),
        P(),
    )
    out_specs = (P("val", "pos", None), P("pos", None, None))
    return jax.shard_map(local, mesh=mesh, in_specs=in_specs, out_specs=out_specs, check_vma=False)
```

```python
import functools
import math

import jax
import jax.numpy as jnp
from jax import lax
from jax.experimental import pallas as pl
from jax.experimental.pallas import tpu as pltpu
from jax.sharding import PartitionSpec as P

HEADS = 8
POWERS = 7
ACTIONS = 32
ITERS = 8
SIZES = (5, 6)
LANES = 128
AHEAD = 8
SMOOTHING = 0.01
F32 = jnp.float32
BF16 = jnp.bfloat16


def dot(a, b):
    return jnp.dot(a, b, preferred_element_type=F32)


def dot_nt(a, b):
    return lax.dot_general(a, b, (((1,), (1,)), ((), ())), preferred_element_type=F32)


def dot_tn(a, b):
    return lax.dot_general(a, b, (((0,), (0,)), ((), ())), preferred_element_type=F32)


def norm(u):
    centre = u - jnp.mean(u, axis=-1, keepdims=True)
    spread = jnp.mean(centre * centre, axis=-1, keepdims=True)
    return centre * lax.rsqrt(spread + 1e-05)


def evaluate_kernel(n_rows, n_blocks, locs, *refs):
    load_ref = refs[0]
    owner_refs = refs[1 : 1 + n_blocks]
    token_refs = refs[1 + n_blocks : 1 + 2 * n_blocks]
    (
        board_ref,
        embed_ref,
        value_ref,
        qkv_ref,
        out_ref,
        up_ref,
        down_ref,
    ) = refs[1 + 3 * n_blocks : 8 + 3 * n_blocks]
    result_ref, token_ref, sum_ref = refs[8 + 3 * n_blocks : 11 + 3 * n_blocks]
    scratch = refs[11 + 3 * n_blocks :]
    pos, me = lax.axis_index("pos"), lax.axis_index("val")
    vocab, width = embed_ref.shape
    pitch = -(-locs // 16) * 16
    places = token_ref.shape[0]
    slots = places // n_rows
    starts, total = [], jnp.int32(0)
    for v in range(n_rows):
        starts.append(total)
        total = total + load_ref[v, pos]
    low = lax.div(me * total + (n_rows - 1), jnp.int32(n_rows))
    high = lax.div((me + 1) * total + (n_rows - 1), jnp.int32(n_rows))
    count = high - low

    def block_of(row):
        return lax.rem(row - me + n_rows, n_rows) if n_blocks == 2 else row

    def owner_at(block, slot):
        if n_blocks == 1:
            return owner_refs[0][block, slot]
        return jnp.where(block == 0, owner_refs[0][0, slot], owner_refs[1][0, slot])

    for b in range(n_blocks):
        part = places // n_blocks
        token_ref[b * part : (b + 1) * part, :] = token_refs[b][...]
    sum_ref[...] = jnp.zeros_like(sum_ref)
    gap = locs // 16 * 16
    for g in range(max(SIZES)):
        for r in scratch[:2]:
            blank = slice(g * pitch + gap, (g + 1) * pitch)
            r[blank] = jnp.zeros_like(r[blank])
    head = width // HEADS
    pair = 2 * head
    key_gap = jnp.zeros((LANES - pitch, pair), BF16)
    head_gap = jnp.zeros((head, LANES), BF16)
    first_half = lax.broadcasted_iota(jnp.int32, (pitch, pair), 1) < head
    first_scale = jnp.where(first_half, 1.0 / 128.0, 0.0).astype(BF16)
    second_scale = jnp.where(first_half, 0.0, 1.0 / 128.0).astype(BF16)
    row_k = lax.broadcasted_iota(jnp.int32, (2 * LANES, pair), 0)
    lane_k = lax.broadcasted_iota(jnp.int32, (2 * LANES, pair), 1)
    ones_block = jnp.where(
        (lax.rem(row_k, jnp.int32(LANES)) < locs) & ((row_k >= LANES) == (lane_k >= head)), 1.0, 0.0
    ).astype(BF16)
    score_scale = head ** (-0.5) * math.log2(math.e)
    selector_row = lax.broadcasted_iota(jnp.int32, (16, max(SIZES) * pitch), 0)
    selector_lane = lax.broadcasted_iota(jnp.int32, (16, max(SIZES) * pitch), 1)
    vocab_ids = lax.broadcasted_iota(jnp.int32, (vocab, locs), 0)

    def group_step(size, group, carry):
        first = group * size
        state_ref, exact_ref, joined_ref, mixed_ref, normed_ref, hidden_ref = scratch
        rows = slice(0, size * pitch)
        at = []
        selector = jnp.where(
            (lax.div(selector_lane, jnp.int32(pitch)) == selector_row)
            & (lax.rem(selector_lane, jnp.int32(pitch)) < locs),
            1.0,
            0.0,
        ).astype(BF16)[:, rows]

        def embed(g):
            item = low + jnp.minimum(first + g, count - 1)
            row, start = jnp.int32(0), jnp.int32(0)
            for v in range(1, n_rows):
                inside = item >= starts[v]
                row = jnp.where(inside, v, row)
                start = jnp.where(inside, starts[v], start)
            slot = item - start
            block = block_of(row)
            place = block * slots + slot
            at.append(place)
            board = lax.div(owner_at(block, slot), jnp.int32(ITERS))
            ids = token_ref[pl.ds(place, 1), :]
            hot = jnp.where(vocab_ids == ids, 1.0, 0.0).astype(BF16)
            exact = (dot_tn(hot, embed_ref[...]) + board_ref[board]).astype(BF16)
            exact_ref[g * pitch : g * pitch + locs, :] = exact
            state_ref[g * pitch : g * pitch + locs, :] = exact.astype(F32)

        def add_sums(lane, array):
            sums = dot(selector, array)
            for g in range(size):
                sum_ref[pl.ds(at[g], 1), lane : lane + sums.shape[1]] = sums[g : g + 1]

        def norm_state(g):
            here = slice(g * pitch, (g + 1) * pitch)
            normed_ref[here] = norm(state_ref[here]).astype(BF16)

        def join():
            joined_ref[rows] = dot(normed_ref[rows], qkv_ref[...]).astype(BF16)

        def score(g, p):
            here = slice(g * pitch, (g + 1) * pitch)
            lane = p * pair
            query = joined_ref[here, lane : lane + pair]
            key = joined_ref[here, width + lane : width + lane + pair]
            turned = jnp.concatenate([key, key_gap], axis=0).T
            keys = jnp.concatenate(
                [
                    jnp.concatenate([turned[:head], head_gap], axis=0),
                    jnp.concatenate([head_gap, turned[head:]], axis=0),
                ],
                axis=1,
            )
            return jnp.exp2(dot(query, keys) * score_scale).astype(BF16)

        def mix(g, p, weights):
            here = slice(g * pitch, (g + 1) * pitch)
            lane = p * pair
            value = joined_ref[here, 2 * width + lane : 2 * width + lane + pair]
            values = jnp.concatenate(
                [value * first_scale, key_gap, value * second_scale, key_gap], axis=0
            )
            both = dot(weights, jnp.concatenate([values, ones_block], axis=1))
            part = (both[:, :pair] / both[:, pair:] * 128.0).astype(BF16)
            mixed_ref[here, lane : lane + pair] = part

        def hide():
            hidden_ref[rows] = state_ref[rows] + dot(mixed_ref[rows], out_ref[...])

        def norm_hidden(g):
            here = slice(g * pitch, (g + 1) * pitch)
            normed_ref[here] = norm(hidden_ref[here]).astype(BF16)

        def feed():
            up = dot(normed_ref[rows], up_ref[...]).astype(BF16)
            inner = up * (
                jnp.asarray(math.sqrt(2.0 / math.pi), BF16)
                + jnp.asarray(math.sqrt(2.0 / math.pi) * 0.044715, BF16) * (up * up)
            )
            half = jnp.asarray(0.5, BF16) * up
            add_sums(2 * width, half + half * jnp.tanh(inner))

        for g in range(size):
            embed(g)
        for g in range(size):
            norm_state(g)
        join()
        order = [(g, p) for g in range(size) for p in range(HEADS // 2)]
        waiting = []
        for here in order + [None] * AHEAD:
            if here is not None:
                waiting.append((here, score(*here)))
            if here is None or len(waiting) > AHEAD:
                ready, weights = waiting.pop(0)
                mix(*ready, weights)
        hide()
        for g in range(size):
            norm_hidden(g)
        add_sums(0, exact_ref[rows])
        add_sums(width, mixed_ref[rows])
        feed()
        return carry

    small, large = SIZES
    steps = lax.div(count + (large - 1), jnp.int32(large))
    fits = steps * small >= count
    for size, chosen in ((small, fits), (large, jnp.logical_not(fits))):
        lax.fori_loop(0, jnp.where(chosen, steps, 0), functools.partial(group_step, size), 0)
    mixed_active = sum_ref[:, width:]
    upper = mixed_active.astype(BF16)
    halves = jnp.concatenate([upper, (mixed_active - upper.astype(F32)).astype(BF16)], axis=0)
    added = dot(halves[:, :width], out_ref[...]) + dot(halves[:, width:], down_ref[...])
    final = sum_ref[:, :width] + (added[:places] + added[places:])
    pooled = norm(final * (1.0 / locs)).astype(BF16)
    raised = jnp.exp(2.0 * dot_nt(value_ref[...], pooled))
    values = raised / jnp.sum(raised, axis=0, keepdims=True)
    lane = lax.broadcasted_iota(jnp.int32, (POWERS, places), 1)
    mine = lane < 0
    for v in range(n_rows):
        slot = lane - block_of(v) * slots
        item = slot + starts[v]
        mine = mine | (
            (slot >= 0) & (slot < load_ref[v, pos]) & (item >= low) & (item < high)
        )
    result_ref[...] = jnp.where(mine, values, 0.0)


def fetch_kernel(n, *refs):
    sources = refs[:n]
    boards_ref, targets = refs[n], refs[n + 1 : 2 * n]
    board_ref, sem = refs[2 * n :]
    copies = [
        pltpu.make_async_copy(source, target, sem.at[i])
        for i, (source, target) in enumerate(zip(sources, (board_ref,) + targets))
    ]
    for copy in copies:
        copy.start()
    copies[0].wait()
    board = board_ref[...].astype(F32)
    for b in range(boards_ref.shape[0]):
        boards_ref[b] = board[:, b, :]
    for copy in copies[1:]:
        copy.wait()


def finish_kernel(n_rows, n_blocks, *refs):
    load_ref = refs[0]
    owner_refs = refs[1 : 1 + n_blocks]
    action_refs = refs[1 + n_blocks : 1 + 2 * n_blocks]
    value_refs = refs[1 + 2 * n_blocks : 1 + 3 * n_blocks]
    state_values_ref, policy_ref, action_ref, value_ref = refs[1 + 3 * n_blocks :]
    pos, me = lax.axis_index("pos"), lax.axis_index("val")
    slots = state_values_ref.shape[2]
    boards = policy_ref.shape[1]
    places = value_ref.shape[0]
    pad = 8
    lane = lax.broadcasted_iota(jnp.int32, (slots, LANES), 1)
    lane_cell = lax.div(lane, jnp.int32(pad))
    slot_down = lax.broadcasted_iota(jnp.int32, (slots, 1), 0)
    square = lax.broadcasted_iota(jnp.int32, (slots, slots), 0) == lax.broadcasted_iota(
        jnp.int32, (slots, slots), 1
    )
    for v in range(n_rows):
        if n_blocks == 1:
            row = jnp.int32(v)
            owners = owner_refs[0][v : v + 1, :]
            actions = [action_refs[0][i, v : v + 1, :] for i in range(POWERS)]
            values = value_refs[0][:, v * slots : (v + 1) * slots]
        else:
            row = lax.rem(me + v, n_rows)
            owners = owner_refs[v][...]
            actions = [action_refs[v][i] for i in range(POWERS)]
            here, there = v * slots, (1 - v) * slots
            values = (
                value_refs[0][:, here : here + slots] + value_refs[1][:, there : there + slots]
            )

        def store(values=values):
            for i in range(POWERS):
                state_values_ref[i] = values[i : i + 1]

        if n_blocks == 1:
            pl.when(me == v)(store)
        elif v == 0:
            store()
        blank = jnp.zeros((1, slots), F32)
        stacked = jnp.concatenate(
            [values, blank] + [a.astype(F32) for a in actions] + [blank], axis=0
        )
        turned = stacked.T
        cell = jnp.sum(jnp.where(square, owners, 0), axis=1, keepdims=True)
        spread = jnp.concatenate([turned[:, :pad]] * (LANES // pad), axis=1)
        chosen = jnp.concatenate([turned[:, pad:]] * (LANES // pad), axis=1).astype(jnp.int32)
        live = (lane_cell == cell) & (slot_down < load_ref[row, pos])
        action_ref[v * slots : (v + 1) * slots, :] = jnp.where(live, chosen, -1)
        value_ref[v * slots : (v + 1) * slots, :] = spread
    action_ids = lax.broadcasted_iota(jnp.int32, (ACTIONS, LANES), 0)
    unit = 16

    def add_slots(step, sums):
        counts, value_sums = sums
        base = step * unit
        for k in range(unit):
            hit = action_ids == action_ref[pl.ds(base + k, 1), :]
            counts = counts + jnp.where(hit, 1.0, 0.0)
            value_sums = value_sums + jnp.where(hit, value_ref[pl.ds(base + k, 1), :], 0.0)
        return counts, value_sums

    sums = (jnp.zeros((ACTIONS, LANES), F32), jnp.zeros((ACTIONS, LANES), F32))
    if places <= 2 * unit:
        for step in range(places // unit):
            sums = add_slots(step, sums)
    else:
        sums = lax.fori_loop(0, places // unit, add_slots, sums)
    counts, value_sums = sums
    visits = jnp.sum(counts, axis=0, keepdims=True)
    totals = jnp.sum(value_sums, axis=0, keepdims=True)
    baseline = (totals + 1.0 / POWERS) / (visits + 1.0)
    payoff = (value_sums + baseline) / (counts + 1.0)
    regrets = jnp.zeros((ACTIONS, LANES), F32)
    average = jnp.zeros((ACTIONS, LANES), F32)
    payoffs = [payoff] + [pltpu.roll(payoff, LANES - t * pad, 1) for t in range(1, ITERS)]
    smoothed = [SMOOTHING * jnp.sum(current, axis=0, keepdims=True) for current in payoffs]
    for t in range(ITERS):
        current = payoffs[t]
        positive = jnp.maximum(regrets, 0.0)
        weight = 1.0 / (jnp.sum(positive, axis=0, keepdims=True) + ACTIONS * SMOOTHING)
        expected = jnp.sum(positive * current, axis=0, keepdims=True) + smoothed[t]
        average = average + (positive + SMOOTHING) * weight
        regrets = regrets + current - expected * weight
    turned = (average / ITERS).T
    for b in range(boards):
        first = b * ITERS * pad
        policy_ref[:, b, :] = turned[first : first + POWERS]


def local(
    send_load,
    tokens,
    owner,
    joint_action,
    board_context,
    tok_embed,
    w_qkv,
    w_attn_out,
    w_up,
    w_down,
    w_value,
):
    n_rows = lax.axis_size("val")
    slots, locs = tokens.shape[1:]
    boards = board_context.shape[0]
    width, hidden_units = w_up.shape
    tokens = tokens.reshape(slots, locs)
    actions = jnp.transpose(joint_action, (2, 0, 1))
    if n_rows == 2:

        def rows_of(array, axis):
            return [array, lax.ppermute(array, "val", [(0, 1), (1, 0)])]

    else:

        def rows_of(array, axis):
            return [lax.all_gather(array, "val", axis=axis, tiled=True)]

    token_blocks, owners, actions = rows_of(tokens, 0), rows_of(owner, 0), rows_of(actions, 1)
    n_blocks = len(owners)
    vmem = pl.BlockSpec(memory_space=pltpu.VMEM)
    smem = pl.BlockSpec(memory_space=pltpu.SMEM)
    hbm = pl.BlockSpec(memory_space=pl.ANY)
    rows = max(SIZES) * (-(-locs // 16) * 16)
    places = n_rows * slots
    inputs = (jnp.transpose(board_context, (1, 0, 2)), tok_embed, w_qkv, w_attn_out)
    held = pl.pallas_call(
        functools.partial(fetch_kernel, len(inputs)),
        out_shape=[pltpu.VMEM((boards, locs, width), F32)]
        + [pltpu.VMEM(w.shape, BF16) for w in inputs[1:]],
        in_specs=[hbm] * len(inputs),
        out_specs=[vmem] * len(inputs),
        scratch_shapes=[
            pltpu.VMEM(inputs[0].shape, BF16),
            pltpu.SemaphoreType.DMA((len(inputs),)),
        ],
        compiler_params=pltpu.CompilerParams(vmem_limit_bytes=58 * 1024 * 1024),
        cost_estimate=pl.CostEstimate(flops=0, bytes_accessed=9000000, transcendentals=0),
        name="fetch",
    )(*inputs)
    values = pl.pallas_call(
        functools.partial(evaluate_kernel, n_rows, n_blocks, locs),
        out_shape=jax.ShapeDtypeStruct((POWERS, places), F32),
        in_specs=[smem] + [smem] * n_blocks + [vmem] * (2 * n_blocks + 7),
        out_specs=vmem,
        scratch_shapes=[
            pltpu.VMEM((places, locs), jnp.int32),
            pltpu.VMEM((places, 2 * width + hidden_units), F32),
        ]
        + [
            pltpu.VMEM((rows, width), F32),
            pltpu.VMEM((rows, width), BF16),
            pltpu.VMEM((rows, 3 * width), BF16),
            pltpu.VMEM((rows, width), BF16),
            pltpu.VMEM((rows, width), BF16),
            pltpu.VMEM((rows, width), F32),
        ],
        compiler_params=pltpu.CompilerParams(vmem_limit_bytes=28 * 1024 * 1024),
        name="evaluate",
    )(send_load, *owners, *token_blocks, *actions, *held[:2], w_value.T, *held[2:], w_up, w_down)
    if n_rows == 2:
        shares = [values, lax.ppermute(values, "val", [(0, 1), (1, 0)])]
    else:
        shares = [lax.psum(values, "val")]
    state_values, policy = pl.pallas_call(
        functools.partial(finish_kernel, n_rows, n_blocks),
        out_shape=(
            jax.ShapeDtypeStruct((POWERS, 1, slots), F32),
            jax.ShapeDtypeStruct((POWERS, boards, ACTIONS), F32),
        ),
        in_specs=[smem] + [vmem] * (3 * n_blocks),
        out_specs=(vmem, vmem),
        scratch_shapes=[
            pltpu.VMEM((places, LANES), jnp.int32),
            pltpu.VMEM((places, LANES), F32),
        ],
        compiler_params=pltpu.CompilerParams(vmem_limit_bytes=16 * 1024 * 1024),
        name="finish",
    )(send_load, *owners, *actions, *shares)
    return (jnp.transpose(state_values, (1, 2, 0)), jnp.transpose(policy, (1, 0, 2)))


def solution(mesh):
    in_specs = (
        P(),
        P("val", "pos", None),
        P("val", "pos"),
        P("val", "pos", None),
        P("pos", None, None),
        P(),
        P(),
        P(),
        P(),
        P(),
        P(),
    )
    out_specs = (P("val", "pos", None), P("pos", None, None))
    return jax.shard_map(local, mesh=mesh, in_specs=in_specs, out_specs=out_specs, check_vma=False)
```

```python
import functools
import math

import jax
import jax.numpy as jnp
from jax import lax
from jax.experimental import pallas as pl
from jax.experimental.pallas import tpu as pltpu
from jax.sharding import PartitionSpec as P

HEADS = 8
POWERS = 7
ACTIONS = 32
ITERS = 8
SIZES = (5, 6)
LANES = 128
PAD = 8
UNIT = 16
AHEAD = 8
SMOOTHING = 0.01
F32 = jnp.float32
BF16 = jnp.bfloat16


def dot(a, b):
    return jnp.dot(a, b, preferred_element_type=F32)


def dot_nt(a, b):
    return lax.dot_general(a, b, (((1,), (1,)), ((), ())), preferred_element_type=F32)


def dot_tn(a, b):
    return lax.dot_general(a, b, (((0,), (0,)), ((), ())), preferred_element_type=F32)


def norm(u):
    centre = u - jnp.mean(u, axis=-1, keepdims=True)
    spread = jnp.mean(centre * centre, axis=-1, keepdims=True)
    return centre * lax.rsqrt(spread + 1e-05)


def evaluate_kernel(n_rows, n_blocks, locs, *refs):
    load_ref = refs[0]
    owner_refs = refs[1 : 1 + n_blocks]
    token_refs = refs[1 + n_blocks : 1 + 2 * n_blocks]
    (
        board_ref,
        embed_ref,
        value_ref,
        qkv_ref,
        out_ref,
        up_ref,
        down_ref,
    ) = refs[1 + 3 * n_blocks : 8 + 3 * n_blocks]
    result_ref, token_ref, sum_ref = refs[8 + 3 * n_blocks : 11 + 3 * n_blocks]
    scratch = refs[11 + 3 * n_blocks :]
    pos, me = lax.axis_index("pos"), lax.axis_index("val")
    vocab, width = embed_ref.shape
    pitch = -(-locs // 16) * 16
    places = token_ref.shape[0]
    slots = places // n_rows
    starts, total = [], jnp.int32(0)
    for v in range(n_rows):
        starts.append(total)
        total = total + load_ref[v, pos]
    low = lax.div(me * total + (n_rows - 1), jnp.int32(n_rows))
    high = lax.div((me + 1) * total + (n_rows - 1), jnp.int32(n_rows))
    count = high - low

    def block_of(row):
        return lax.rem(row - me + n_rows, n_rows) if n_blocks == 2 else row

    def owner_at(block, slot):
        if n_blocks == 1:
            return owner_refs[0][block, slot]
        return jnp.where(block == 0, owner_refs[0][0, slot], owner_refs[1][0, slot])

    for b in range(n_blocks):
        part = places // n_blocks
        token_ref[b * part : (b + 1) * part, :] = token_refs[b][...]
    sum_ref[...] = jnp.zeros_like(sum_ref)
    gap = locs // 16 * 16
    for g in range(max(SIZES)):
        for r in scratch[:2]:
            blank = slice(g * pitch + gap, (g + 1) * pitch)
            r[blank] = jnp.zeros_like(r[blank])
    head = width // HEADS
    pair = 2 * head
    key_gap = jnp.zeros((LANES - pitch, pair), BF16)
    head_gap = jnp.zeros((head, LANES), BF16)
    first_half = lax.broadcasted_iota(jnp.int32, (pitch, pair), 1) < head
    first_scale = jnp.where(first_half, 1.0 / 128.0, 0.0).astype(BF16)
    second_scale = jnp.where(first_half, 0.0, 1.0 / 128.0).astype(BF16)
    row_k = lax.broadcasted_iota(jnp.int32, (2 * LANES, pair), 0)
    lane_k = lax.broadcasted_iota(jnp.int32, (2 * LANES, pair), 1)
    ones_block = jnp.where(
        (lax.rem(row_k, jnp.int32(LANES)) < locs) & ((row_k >= LANES) == (lane_k >= head)), 1.0, 0.0
    ).astype(BF16)
    score_scale = head ** (-0.5) * math.log2(math.e)
    selector_row = lax.broadcasted_iota(jnp.int32, (16, max(SIZES) * pitch), 0)
    selector_lane = lax.broadcasted_iota(jnp.int32, (16, max(SIZES) * pitch), 1)
    vocab_ids = lax.broadcasted_iota(jnp.int32, (vocab, locs), 0)

    def group_step(size, group, carry):
        first = group * size
        state_ref, exact_ref, joined_ref, mixed_ref, normed_ref, hidden_ref = scratch
        rows = slice(0, size * pitch)
        at = []
        selector = jnp.where(
            (lax.div(selector_lane, jnp.int32(pitch)) == selector_row)
            & (lax.rem(selector_lane, jnp.int32(pitch)) < locs),
            1.0,
            0.0,
        ).astype(BF16)[:, rows]

        def embed(g):
            item = low + jnp.minimum(first + g, count - 1)
            row, start = jnp.int32(0), jnp.int32(0)
            for v in range(1, n_rows):
                inside = item >= starts[v]
                row = jnp.where(inside, v, row)
                start = jnp.where(inside, starts[v], start)
            slot = item - start
            block = block_of(row)
            place = block * slots + slot
            at.append(place)
            board = lax.div(owner_at(block, slot), jnp.int32(ITERS))
            ids = token_ref[pl.ds(place, 1), :]
            hot = jnp.where(vocab_ids == ids, 1.0, 0.0).astype(BF16)
            exact = (dot_tn(hot, embed_ref[...]) + board_ref[board]).astype(BF16)
            exact_ref[g * pitch : g * pitch + locs, :] = exact
            state_ref[g * pitch : g * pitch + locs, :] = exact.astype(F32)

        def add_sums(lane, array):
            sums = dot(selector, array)
            for g in range(size):
                sum_ref[pl.ds(at[g], 1), lane : lane + sums.shape[1]] = sums[g : g + 1]

        def norm_state(g):
            here = slice(g * pitch, (g + 1) * pitch)
            normed_ref[here] = norm(state_ref[here]).astype(BF16)

        def join():
            joined_ref[rows] = dot(normed_ref[rows], qkv_ref[...]).astype(BF16)

        def score(g, p):
            here = slice(g * pitch, (g + 1) * pitch)
            lane = p * pair
            query = joined_ref[here, lane : lane + pair]
            key = joined_ref[here, width + lane : width + lane + pair]
            turned = jnp.concatenate([key, key_gap], axis=0).T
            keys = jnp.concatenate(
                [
                    jnp.concatenate([turned[:head], head_gap], axis=0),
                    jnp.concatenate([head_gap, turned[head:]], axis=0),
                ],
                axis=1,
            )
            return jnp.exp2(dot(query, keys) * score_scale).astype(BF16)

        def mix(g, p, weights):
            here = slice(g * pitch, (g + 1) * pitch)
            lane = p * pair
            value = joined_ref[here, 2 * width + lane : 2 * width + lane + pair]
            values = jnp.concatenate(
                [value * first_scale, key_gap, value * second_scale, key_gap], axis=0
            )
            both = dot(weights, jnp.concatenate([values, ones_block], axis=1))
            part = (both[:, :pair] / both[:, pair:] * 128.0).astype(BF16)
            mixed_ref[here, lane : lane + pair] = part

        def hide():
            hidden_ref[rows] = state_ref[rows] + dot(mixed_ref[rows], out_ref[...])

        def norm_hidden(g):
            here = slice(g * pitch, (g + 1) * pitch)
            normed_ref[here] = norm(hidden_ref[here]).astype(BF16)

        def feed():
            up = dot(normed_ref[rows], up_ref[...]).astype(BF16)
            inner = up * (
                jnp.asarray(math.sqrt(2.0 / math.pi), BF16)
                + jnp.asarray(math.sqrt(2.0 / math.pi) * 0.044715, BF16) * (up * up)
            )
            half = jnp.asarray(0.5, BF16) * up
            add_sums(2 * width, half + half * jnp.tanh(inner))

        for g in range(size):
            embed(g)
        for g in range(size):
            norm_state(g)
        join()
        order = [(g, p) for g in range(size) for p in range(HEADS // 2)]
        waiting = []
        for here in order + [None] * AHEAD:
            if here is not None:
                waiting.append((here, score(*here)))
            if here is None or len(waiting) > AHEAD:
                ready, weights = waiting.pop(0)
                mix(*ready, weights)
        hide()
        for g in range(size):
            norm_hidden(g)
        add_sums(0, exact_ref[rows])
        add_sums(width, mixed_ref[rows])
        feed()
        return carry

    small, large = SIZES
    steps = lax.div(count + (large - 1), jnp.int32(large))
    fits = steps * small >= count
    for size, chosen in ((small, fits), (large, jnp.logical_not(fits))):
        lax.fori_loop(0, jnp.where(chosen, steps, 0), functools.partial(group_step, size), 0)
    mixed_active = sum_ref[:, width:]
    upper = mixed_active.astype(BF16)
    halves = jnp.concatenate([upper, (mixed_active - upper.astype(F32)).astype(BF16)], axis=0)
    added = dot(halves[:, :width], out_ref[...]) + dot(halves[:, width:], down_ref[...])
    final = sum_ref[:, :width] + (added[:places] + added[places:])
    pooled = norm(final * (1.0 / locs)).astype(BF16)
    raised = jnp.exp(2.0 * dot_nt(value_ref[...], pooled))
    values = raised / jnp.sum(raised, axis=0, keepdims=True)
    lane = lax.broadcasted_iota(jnp.int32, (POWERS, places), 1)
    mine = lane < 0
    for v in range(n_rows):
        slot = lane - block_of(v) * slots
        item = slot + starts[v]
        mine = mine | (
            (slot >= 0) & (slot < load_ref[v, pos]) & (item >= low) & (item < high)
        )
    result_ref[...] = jnp.where(mine, values, 0.0)


def fetch_kernel(n, *refs):
    sources = refs[:n]
    boards_ref, targets = refs[n], refs[n + 1 : 2 * n]
    board_ref, sem = refs[2 * n :]
    copies = [
        pltpu.make_async_copy(source, target, sem.at[i])
        for i, (source, target) in enumerate(zip(sources, (board_ref,) + targets))
    ]
    for copy in copies:
        copy.start()
    copies[0].wait()
    board = board_ref[...].astype(F32)
    for b in range(boards_ref.shape[0]):
        boards_ref[b] = board[:, b, :]
    for copy in copies[1:]:
        copy.wait()


def spread_powers(values):
    blank = jnp.zeros((PAD - values.shape[0], values.shape[1]), F32)
    turned = jnp.concatenate([values, blank], axis=0).T
    return jnp.concatenate([turned] * (LANES // PAD), axis=1)


def tally_kernel(n_rows, n_blocks, *refs):
    load_ref = refs[0]
    owner_refs = refs[1 : 1 + n_blocks]
    action_refs = refs[1 + n_blocks : 1 + 2 * n_blocks]
    value_ref, chosen_ref, count_ref, share_ref, spread_ref = refs[1 + 2 * n_blocks :]
    pos, me = lax.axis_index("pos"), lax.axis_index("val")
    places = chosen_ref.shape[0]
    slots = places // n_rows
    lane_cell = lax.div(lax.broadcasted_iota(jnp.int32, (slots, LANES), 1), jnp.int32(PAD))
    slot_down = lax.broadcasted_iota(jnp.int32, (slots, 1), 0)
    square = lax.broadcasted_iota(jnp.int32, (slots, slots), 0) == lax.broadcasted_iota(
        jnp.int32, (slots, slots), 1
    )
    if n_blocks == 2:
        spread_ref[...] = spread_powers(value_ref[...])
    for v in range(n_rows):
        if n_blocks == 1:
            row = jnp.int32(v)
            owners = owner_refs[0][v : v + 1, :]
            actions = [action_refs[0][i, v : v + 1, :] for i in range(POWERS)]
        else:
            row = lax.rem(me + v, n_rows)
            owners = owner_refs[v][...]
            actions = [action_refs[v][i] for i in range(POWERS)]
        cell = jnp.sum(jnp.where(square, owners, 0), axis=1, keepdims=True)
        spread = spread_powers(jnp.concatenate([a.astype(F32) for a in actions], axis=0))
        live = (lane_cell == cell) & (slot_down < load_ref[row, pos])
        chosen_ref[v * slots : (v + 1) * slots, :] = jnp.where(live, spread.astype(jnp.int32), -1)
    action_ids = lax.broadcasted_iota(jnp.int32, (ACTIONS, LANES), 0)

    def add_slots(step, sums):
        counts, shares = sums
        base = step * UNIT
        for k in range(UNIT):
            hit = action_ids == chosen_ref[pl.ds(base + k, 1), :]
            counts = counts + jnp.where(hit, 1.0, 0.0)
            if n_blocks == 2:
                shares = shares + jnp.where(hit, spread_ref[pl.ds(base + k, 1), :], 0.0)
        return counts, shares

    nothing = jnp.zeros((ACTIONS, LANES), F32)
    count_ref[...], share_ref[...] = over_slots(places, add_slots, (nothing, nothing))


def over_slots(places, add_slots, sums):
    if places > 2 * UNIT:
        return lax.fori_loop(0, places // UNIT, add_slots, sums)
    for step in range(places // UNIT):
        sums = add_slots(step, sums)
    return sums


def finish_kernel(n_rows, n_blocks, *refs):
    value_refs = refs[:n_blocks]
    chosen_ref, count_ref, share_ref, state_values_ref, policy_ref, spread_ref = refs[n_blocks:]
    slots = state_values_ref.shape[2]
    boards = policy_ref.shape[1]
    places = chosen_ref.shape[0]
    arrived = value_refs[-1][...]
    if n_blocks == 2:
        values = value_refs[0][:, :slots] + arrived[:, slots:]
        spread = spread_powers(arrived)
        spread_ref[:slots] = spread[slots:]
        spread_ref[slots:] = spread[:slots]
    else:
        me = lax.axis_index("val")
        values = arrived[:, :slots]
        for v in range(1, n_rows):
            values = jnp.where(me == v, arrived[:, v * slots : (v + 1) * slots], values)
        spread_ref[...] = spread_powers(arrived)
    for i in range(POWERS):
        state_values_ref[i] = values[i : i + 1]
    action_ids = lax.broadcasted_iota(jnp.int32, (ACTIONS, LANES), 0)

    def add_slots(step, sums):
        base = step * UNIT
        for k in range(UNIT):
            hit = action_ids == chosen_ref[pl.ds(base + k, 1), :]
            sums = sums + jnp.where(hit, spread_ref[pl.ds(base + k, 1), :], 0.0)
        return sums

    counts = count_ref[...]
    value_sums = over_slots(places, add_slots, share_ref[...])
    visits = jnp.sum(counts, axis=0, keepdims=True)
    totals = jnp.sum(value_sums, axis=0, keepdims=True)
    baseline = (totals + 1.0 / POWERS) / (visits + 1.0)
    payoff = (value_sums + baseline) / (counts + 1.0)
    payoffs = [payoff] + [pltpu.roll(payoff, LANES - t * PAD, 1) for t in range(1, ITERS)]
    smoothed = [SMOOTHING * jnp.sum(current, axis=0, keepdims=True) for current in payoffs]
    regrets = jnp.zeros((ACTIONS, LANES), F32)
    average = jnp.zeros((ACTIONS, LANES), F32)
    for t in range(ITERS):
        current = payoffs[t]
        positive = jnp.maximum(regrets, 0.0)
        weight = 1.0 / (jnp.sum(positive, axis=0, keepdims=True) + ACTIONS * SMOOTHING)
        expected = jnp.sum(positive * current, axis=0, keepdims=True) + smoothed[t]
        average = average + (positive + SMOOTHING) * weight
        regrets = regrets + current - expected * weight
    turned = (average / ITERS).T
    for b in range(boards):
        first = b * ITERS * PAD
        policy_ref[:, b, :] = turned[first : first + POWERS]


def local(
    send_load,
    tokens,
    owner,
    joint_action,
    board_context,
    tok_embed,
    w_qkv,
    w_attn_out,
    w_up,
    w_down,
    w_value,
):
    n_rows = lax.axis_size("val")
    slots, locs = tokens.shape[1:]
    boards = board_context.shape[0]
    width, hidden_units = w_up.shape
    tokens = tokens.reshape(slots, locs)
    actions = jnp.transpose(joint_action, (2, 0, 1))
    if n_rows == 2:

        def rows_of(array, axis):
            return [array, lax.ppermute(array, "val", [(0, 1), (1, 0)])]

    else:

        def rows_of(array, axis):
            return [lax.all_gather(array, "val", axis=axis, tiled=True)]

    token_blocks, owners, actions = rows_of(tokens, 0), rows_of(owner, 0), rows_of(actions, 1)
    n_blocks = len(owners)
    vmem = pl.BlockSpec(memory_space=pltpu.VMEM)
    smem = pl.BlockSpec(memory_space=pltpu.SMEM)
    hbm = pl.BlockSpec(memory_space=pl.ANY)
    rows = max(SIZES) * (-(-locs // 16) * 16)
    places = n_rows * slots
    inputs = (jnp.transpose(board_context, (1, 0, 2)), tok_embed, w_qkv, w_attn_out)
    held = pl.pallas_call(
        functools.partial(fetch_kernel, len(inputs)),
        out_shape=[pltpu.VMEM((boards, locs, width), F32)]
        + [pltpu.VMEM(w.shape, BF16) for w in inputs[1:]],
        in_specs=[hbm] * len(inputs),
        out_specs=[vmem] * len(inputs),
        scratch_shapes=[
            pltpu.VMEM(inputs[0].shape, BF16),
            pltpu.SemaphoreType.DMA((len(inputs),)),
        ],
        compiler_params=pltpu.CompilerParams(vmem_limit_bytes=58 * 1024 * 1024),
        cost_estimate=pl.CostEstimate(flops=0, bytes_accessed=9000000, transcendentals=0),
        name="fetch",
    )(*inputs)
    values = pl.pallas_call(
        functools.partial(evaluate_kernel, n_rows, n_blocks, locs),
        out_shape=jax.ShapeDtypeStruct((POWERS, places), F32),
        in_specs=[smem] + [smem] * n_blocks + [vmem] * (2 * n_blocks + 7),
        out_specs=vmem,
        scratch_shapes=[
            pltpu.VMEM((places, locs), jnp.int32),
            pltpu.VMEM((places, 2 * width + hidden_units), F32),
        ]
        + [
            pltpu.VMEM((rows, width), F32),
            pltpu.VMEM((rows, width), BF16),
            pltpu.VMEM((rows, 3 * width), BF16),
            pltpu.VMEM((rows, width), BF16),
            pltpu.VMEM((rows, width), BF16),
            pltpu.VMEM((rows, width), F32),
        ],
        compiler_params=pltpu.CompilerParams(vmem_limit_bytes=28 * 1024 * 1024),
        name="evaluate",
    )(send_load, *owners, *token_blocks, *actions, *held[:2], w_value.T, *held[2:], w_up, w_down)
    if n_rows == 2:
        shares = [values, lax.ppermute(values, "val", [(0, 1), (1, 0)])]
    else:
        shares = [lax.psum(values, "val")]
    chosen, counts, own_sums = pl.pallas_call(
        functools.partial(tally_kernel, n_rows, n_blocks),
        out_shape=(
            jax.ShapeDtypeStruct((places, LANES), jnp.int32),
            jax.ShapeDtypeStruct((ACTIONS, LANES), F32),
            jax.ShapeDtypeStruct((ACTIONS, LANES), F32),
        ),
        in_specs=[smem] + [vmem] * (2 * n_blocks + 1),
        out_specs=(vmem, vmem, vmem),
        scratch_shapes=[pltpu.VMEM((places, LANES), F32)],
        compiler_params=pltpu.CompilerParams(vmem_limit_bytes=16 * 1024 * 1024),
        cost_estimate=pl.CostEstimate(flops=0, bytes_accessed=4000000, transcendentals=0),
        name="tally",
    )(send_load, *owners, *actions, values)
    state_values, policy = pl.pallas_call(
        functools.partial(finish_kernel, n_rows, n_blocks),
        out_shape=(
            jax.ShapeDtypeStruct((POWERS, 1, slots), F32),
            jax.ShapeDtypeStruct((POWERS, boards, ACTIONS), F32),
        ),
        in_specs=[vmem] * (n_blocks + 3),
        out_specs=(vmem, vmem),
        scratch_shapes=[pltpu.VMEM((places, LANES), F32)],
        compiler_params=pltpu.CompilerParams(vmem_limit_bytes=16 * 1024 * 1024),
        name="finish",
    )(*shares, chosen, counts, own_sums)
    return (jnp.transpose(state_values, (1, 2, 0)), jnp.transpose(policy, (1, 0, 2)))


def solution(mesh):
    in_specs = (
        P(),
        P("val", "pos", None),
        P("val", "pos"),
        P("val", "pos", None),
        P("pos", None, None),
        P(),
        P(),
        P(),
        P(),
        P(),
        P(),
    )
    out_specs = (P("val", "pos", None), P("pos", None, None))
    return jax.shard_map(local, mesh=mesh, in_specs=in_specs, out_specs=out_specs, check_vma=False)
```

```python
import functools
import math

import jax
import jax.numpy as jnp
from jax import lax
from jax.experimental import pallas as pl
from jax.experimental.pallas import tpu as pltpu
from jax.sharding import PartitionSpec as P

HEADS = 8
POWERS = 7
ACTIONS = 32
ITERS = 8
SIZES = (8, 9, 10, 11, 12)
LANES = 128
PAD = 8
UNIT = 16
AHEAD = 8
SMOOTHING = 0.01
F32 = jnp.float32
BF16 = jnp.bfloat16


def dot(a, b):
    return jnp.dot(a, b, preferred_element_type=F32)


def dot_nt(a, b):
    return lax.dot_general(a, b, (((1,), (1,)), ((), ())), preferred_element_type=F32)


def dot_tn(a, b):
    return lax.dot_general(a, b, (((0,), (0,)), ((), ())), preferred_element_type=F32)


def norm(u):
    centre = u - jnp.mean(u, axis=-1, keepdims=True)
    spread = jnp.mean(centre * centre, axis=-1, keepdims=True)
    return centre * lax.rsqrt(spread + 1e-05)


def evaluate_kernel(n_rows, n_blocks, locs, *refs):
    load_ref = refs[0]
    owner_refs = refs[1 : 1 + n_blocks]
    token_refs = refs[1 + n_blocks : 1 + 2 * n_blocks]
    (
        board_ref,
        embed_ref,
        value_ref,
        qkv_ref,
        out_ref,
        up_ref,
        down_ref,
    ) = refs[1 + 3 * n_blocks : 8 + 3 * n_blocks]
    result_ref, token_ref, sum_ref = refs[8 + 3 * n_blocks : 11 + 3 * n_blocks]
    scratch = refs[11 + 3 * n_blocks :]
    pos, me = lax.axis_index("pos"), lax.axis_index("val")
    vocab, width = embed_ref.shape
    pitch = -(-locs // 16) * 16
    places = token_ref.shape[0]
    slots = places // n_rows
    starts, total = [], jnp.int32(0)
    for v in range(n_rows):
        starts.append(total)
        total = total + load_ref[v, pos]
    low = lax.div(me * total + (n_rows - 1), jnp.int32(n_rows))
    high = lax.div((me + 1) * total + (n_rows - 1), jnp.int32(n_rows))
    count = high - low

    def block_of(row):
        return lax.rem(row - me + n_rows, n_rows) if n_blocks == 2 else row

    def owner_at(block, slot):
        if n_blocks == 1:
            return owner_refs[0][block, slot]
        return jnp.where(block == 0, owner_refs[0][0, slot], owner_refs[1][0, slot])

    for b in range(n_blocks):
        part = places // n_blocks
        token_ref[b * part : (b + 1) * part, :] = token_refs[b][...]
    sum_ref[...] = jnp.zeros_like(sum_ref)
    gap = locs // 16 * 16
    for g in range(max(SIZES)):
        for r in scratch[:2]:
            blank = slice(g * pitch + gap, (g + 1) * pitch)
            r[blank] = jnp.zeros_like(r[blank])
    head = width // HEADS
    pair = 2 * head
    key_gap = jnp.zeros((LANES - pitch, pair), BF16)
    head_gap = jnp.zeros((head, LANES), BF16)
    first_half = lax.broadcasted_iota(jnp.int32, (pitch, pair), 1) < head
    first_scale = jnp.where(first_half, 1.0 / 128.0, 0.0).astype(BF16)
    second_scale = jnp.where(first_half, 0.0, 1.0 / 128.0).astype(BF16)
    row_k = lax.broadcasted_iota(jnp.int32, (2 * LANES, pair), 0)
    lane_k = lax.broadcasted_iota(jnp.int32, (2 * LANES, pair), 1)
    ones_block = jnp.where(
        (lax.rem(row_k, jnp.int32(LANES)) < locs) & ((row_k >= LANES) == (lane_k >= head)), 1.0, 0.0
    ).astype(BF16)
    score_scale = head ** (-0.5) * math.log2(math.e)
    selector_row = lax.broadcasted_iota(jnp.int32, (16, max(SIZES) * pitch), 0)
    selector_lane = lax.broadcasted_iota(jnp.int32, (16, max(SIZES) * pitch), 1)
    vocab_ids = lax.broadcasted_iota(jnp.int32, (vocab, locs), 0)

    def group_step(size, group, carry):
        first = group * size
        state_ref, exact_ref, joined_ref, mixed_ref, normed_ref, hidden_ref = scratch
        rows = slice(0, size * pitch)
        at = []
        selector = jnp.where(
            (lax.div(selector_lane, jnp.int32(pitch)) == selector_row)
            & (lax.rem(selector_lane, jnp.int32(pitch)) < locs),
            1.0,
            0.0,
        ).astype(BF16)[:, rows]

        def embed(g):
            item = low + jnp.minimum(first + g, count - 1)
            row, start = jnp.int32(0), jnp.int32(0)
            for v in range(1, n_rows):
                inside = item >= starts[v]
                row = jnp.where(inside, v, row)
                start = jnp.where(inside, starts[v], start)
            slot = item - start
            block = block_of(row)
            place = block * slots + slot
            at.append(place)
            board = lax.div(owner_at(block, slot), jnp.int32(ITERS))
            ids = token_ref[pl.ds(place, 1), :]
            hot = jnp.where(vocab_ids == ids, 1.0, 0.0).astype(BF16)
            exact = (dot_tn(hot, embed_ref[...]) + board_ref[board]).astype(BF16)
            exact_ref[g * pitch : g * pitch + locs, :] = exact
            state_ref[g * pitch : g * pitch + locs, :] = exact.astype(F32)

        def add_sums(lane, array):
            sums = dot(selector, array)
            for g in range(size):
                sum_ref[pl.ds(at[g], 1), lane : lane + sums.shape[1]] = sums[g : g + 1]

        def norm_state(g):
            here = slice(g * pitch, (g + 1) * pitch)
            normed_ref[here] = norm(state_ref[here]).astype(BF16)

        def join():
            joined_ref[rows] = dot(normed_ref[rows], qkv_ref[...]).astype(BF16)

        def score(g, p):
            here = slice(g * pitch, (g + 1) * pitch)
            lane = p * pair
            query = joined_ref[here, lane : lane + pair]
            key = joined_ref[here, width + lane : width + lane + pair]
            turned = jnp.concatenate([key, key_gap], axis=0).T
            keys = jnp.concatenate(
                [
                    jnp.concatenate([turned[:head], head_gap], axis=0),
                    jnp.concatenate([head_gap, turned[head:]], axis=0),
                ],
                axis=1,
            )
            return jnp.exp2(dot(query, keys) * score_scale).astype(BF16)

        def mix(g, p, weights):
            here = slice(g * pitch, (g + 1) * pitch)
            lane = p * pair
            value = joined_ref[here, 2 * width + lane : 2 * width + lane + pair]
            values = jnp.concatenate(
                [value * first_scale, key_gap, value * second_scale, key_gap], axis=0
            )
            both = dot(weights, jnp.concatenate([values, ones_block], axis=1))
            part = (both[:, :pair] / both[:, pair:] * 128.0).astype(BF16)
            mixed_ref[here, lane : lane + pair] = part

        def hide():
            hidden_ref[rows] = state_ref[rows] + dot(mixed_ref[rows], out_ref[...])

        def norm_hidden(g):
            here = slice(g * pitch, (g + 1) * pitch)
            normed_ref[here] = norm(hidden_ref[here]).astype(BF16)

        def feed():
            up = dot(normed_ref[rows], up_ref[...]).astype(BF16)
            inner = up * (
                jnp.asarray(math.sqrt(2.0 / math.pi), BF16)
                + jnp.asarray(math.sqrt(2.0 / math.pi) * 0.044715, BF16) * (up * up)
            )
            half = jnp.asarray(0.5, BF16) * up
            add_sums(2 * width, half + half * jnp.tanh(inner))

        for g in range(size):
            embed(g)
        for g in range(size):
            norm_state(g)
        join()
        order = [(g, p) for g in range(size) for p in range(HEADS // 2)]
        waiting = []
        for here in order + [None] * AHEAD:
            if here is not None:
                waiting.append((here, score(*here)))
            if here is None or len(waiting) > AHEAD:
                ready, weights = waiting.pop(0)
                mix(*ready, weights)
        hide()
        for g in range(size):
            norm_hidden(g)
        add_sums(0, exact_ref[rows])
        add_sums(width, mixed_ref[rows])
        feed()
        return carry

    below = 0
    for size in SIZES[1:]:
        fits = (count > below) & (count <= size)
        lax.fori_loop(0, jnp.where(fits, 1, 0), functools.partial(group_step, size), 0)
        below = size
    size = SIZES[0]
    steps = jnp.where(count > below, lax.div(count + (size - 1), jnp.int32(size)), 0)
    lax.fori_loop(0, steps, functools.partial(group_step, size), 0)
    mixed_active = sum_ref[:, width:]
    upper = mixed_active.astype(BF16)
    halves = jnp.concatenate([upper, (mixed_active - upper.astype(F32)).astype(BF16)], axis=0)
    added = dot(halves[:, :width], out_ref[...]) + dot(halves[:, width:], down_ref[...])
    final = sum_ref[:, :width] + (added[:places] + added[places:])
    pooled = norm(final * (1.0 / locs)).astype(BF16)
    raised = jnp.exp(2.0 * dot_nt(value_ref[...], pooled))
    values = raised / jnp.sum(raised, axis=0, keepdims=True)
    lane = lax.broadcasted_iota(jnp.int32, (POWERS, places), 1)
    mine = lane < 0
    for v in range(n_rows):
        slot = lane - block_of(v) * slots
        item = slot + starts[v]
        mine = mine | (
            (slot >= 0) & (slot < load_ref[v, pos]) & (item >= low) & (item < high)
        )
    result_ref[...] = jnp.where(mine, values, 0.0)


def fetch_kernel(n, *refs):
    sources = refs[:n]
    boards_ref, targets = refs[n], refs[n + 1 : 2 * n]
    board_ref, sem = refs[2 * n :]
    copies = [
        pltpu.make_async_copy(source, target, sem.at[i])
        for i, (source, target) in enumerate(zip(sources, (board_ref,) + targets))
    ]
    for copy in copies:
        copy.start()
    copies[0].wait()
    board = board_ref[...].astype(F32)
    for b in range(boards_ref.shape[0]):
        boards_ref[b] = board[:, b, :]
    for copy in copies[1:]:
        copy.wait()


def spread_powers(values):
    blank = jnp.zeros((PAD - values.shape[0], values.shape[1]), F32)
    turned = jnp.concatenate([values, blank], axis=0).T
    return jnp.concatenate([turned] * (LANES // PAD), axis=1)


def tally_kernel(n_rows, n_blocks, *refs):
    load_ref = refs[0]
    owner_refs = refs[1 : 1 + n_blocks]
    action_refs = refs[1 + n_blocks : 1 + 2 * n_blocks]
    value_ref, chosen_ref, count_ref, share_ref, spread_ref = refs[1 + 2 * n_blocks :]
    pos, me = lax.axis_index("pos"), lax.axis_index("val")
    places = chosen_ref.shape[0]
    slots = places // n_rows
    lane_cell = lax.div(lax.broadcasted_iota(jnp.int32, (slots, LANES), 1), jnp.int32(PAD))
    slot_down = lax.broadcasted_iota(jnp.int32, (slots, 1), 0)
    square = lax.broadcasted_iota(jnp.int32, (slots, slots), 0) == lax.broadcasted_iota(
        jnp.int32, (slots, slots), 1
    )
    if n_blocks == 2:
        spread_ref[...] = spread_powers(value_ref[...])
    for v in range(n_rows):
        if n_blocks == 1:
            row = jnp.int32(v)
            owners = owner_refs[0][v : v + 1, :]
            actions = [action_refs[0][i, v : v + 1, :] for i in range(POWERS)]
        else:
            row = lax.rem(me + v, n_rows)
            owners = owner_refs[v][...]
            actions = [action_refs[v][i] for i in range(POWERS)]
        cell = jnp.sum(jnp.where(square, owners, 0), axis=1, keepdims=True)
        spread = spread_powers(jnp.concatenate([a.astype(F32) for a in actions], axis=0))
        live = (lane_cell == cell) & (slot_down < load_ref[row, pos])
        chosen_ref[v * slots : (v + 1) * slots, :] = jnp.where(live, spread.astype(jnp.int32), -1)
    action_ids = lax.broadcasted_iota(jnp.int32, (ACTIONS, LANES), 0)

    def add_slots(step, sums):
        counts, shares = sums
        base = step * UNIT
        for k in range(UNIT):
            hit = action_ids == chosen_ref[pl.ds(base + k, 1), :]
            counts = counts + jnp.where(hit, 1.0, 0.0)
            if n_blocks == 2:
                shares = shares + jnp.where(hit, spread_ref[pl.ds(base + k, 1), :], 0.0)
        return counts, shares

    nothing = jnp.zeros((ACTIONS, LANES), F32)
    count_ref[...], share_ref[...] = over_slots(places, add_slots, (nothing, nothing))


def over_slots(places, add_slots, sums):
    if places > 2 * UNIT:
        return lax.fori_loop(0, places // UNIT, add_slots, sums)
    for step in range(places // UNIT):
        sums = add_slots(step, sums)
    return sums


def finish_kernel(n_rows, n_blocks, *refs):
    value_refs = refs[:n_blocks]
    chosen_ref, count_ref, share_ref, state_values_ref, policy_ref, spread_ref = refs[n_blocks:]
    slots = state_values_ref.shape[2]
    boards = policy_ref.shape[1]
    places = chosen_ref.shape[0]
    arrived = value_refs[-1][...]
    if n_blocks == 2:
        values = value_refs[0][:, :slots] + arrived[:, slots:]
        spread = spread_powers(arrived)
        spread_ref[:slots] = spread[slots:]
        spread_ref[slots:] = spread[:slots]
    else:
        me = lax.axis_index("val")
        values = arrived[:, :slots]
        for v in range(1, n_rows):
            values = jnp.where(me == v, arrived[:, v * slots : (v + 1) * slots], values)
        spread_ref[...] = spread_powers(arrived)
    for i in range(POWERS):
        state_values_ref[i] = values[i : i + 1]
    action_ids = lax.broadcasted_iota(jnp.int32, (ACTIONS, LANES), 0)

    def add_slots(step, sums):
        base = step * UNIT
        for k in range(UNIT):
            hit = action_ids == chosen_ref[pl.ds(base + k, 1), :]
            sums = sums + jnp.where(hit, spread_ref[pl.ds(base + k, 1), :], 0.0)
        return sums

    counts = count_ref[...]
    value_sums = over_slots(places, add_slots, share_ref[...])
    visits = jnp.sum(counts, axis=0, keepdims=True)
    totals = jnp.sum(value_sums, axis=0, keepdims=True)
    baseline = (totals + 1.0 / POWERS) / (visits + 1.0)
    payoff = (value_sums + baseline) / (counts + 1.0)
    payoffs = [payoff] + [pltpu.roll(payoff, LANES - t * PAD, 1) for t in range(1, ITERS)]
    smoothed = [SMOOTHING * jnp.sum(current, axis=0, keepdims=True) for current in payoffs]
    regrets = jnp.zeros((ACTIONS, LANES), F32)
    average = jnp.zeros((ACTIONS, LANES), F32)
    for t in range(ITERS):
        current = payoffs[t]
        positive = jnp.maximum(regrets, 0.0)
        weight = 1.0 / (jnp.sum(positive, axis=0, keepdims=True) + ACTIONS * SMOOTHING)
        expected = jnp.sum(positive * current, axis=0, keepdims=True) + smoothed[t]
        average = average + (positive + SMOOTHING) * weight
        regrets = regrets + current - expected * weight
    turned = (average / ITERS).T
    for b in range(boards):
        first = b * ITERS * PAD
        policy_ref[:, b, :] = turned[first : first + POWERS]


def local(
    send_load,
    tokens,
    owner,
    joint_action,
    board_context,
    tok_embed,
    w_qkv,
    w_attn_out,
    w_up,
    w_down,
    w_value,
):
    n_rows = lax.axis_size("val")
    slots, locs = tokens.shape[1:]
    boards = board_context.shape[0]
    width, hidden_units = w_up.shape
    tokens = tokens.reshape(slots, locs)
    actions = jnp.transpose(joint_action, (2, 0, 1))
    if n_rows == 2:

        def rows_of(array, axis):
            return [array, lax.ppermute(array, "val", [(0, 1), (1, 0)])]

    else:

        def rows_of(array, axis):
            return [lax.all_gather(array, "val", axis=axis, tiled=True)]

    token_blocks, owners, actions = rows_of(tokens, 0), rows_of(owner, 0), rows_of(actions, 1)
    n_blocks = len(owners)
    vmem = pl.BlockSpec(memory_space=pltpu.VMEM)
    smem = pl.BlockSpec(memory_space=pltpu.SMEM)
    hbm = pl.BlockSpec(memory_space=pl.ANY)
    rows = max(SIZES) * (-(-locs // 16) * 16)
    places = n_rows * slots
    inputs = (jnp.transpose(board_context, (1, 0, 2)), tok_embed, w_qkv, w_attn_out)
    held = pl.pallas_call(
        functools.partial(fetch_kernel, len(inputs)),
        out_shape=[pltpu.VMEM((boards, locs, width), F32)]
        + [pltpu.VMEM(w.shape, BF16) for w in inputs[1:]],
        in_specs=[hbm] * len(inputs),
        out_specs=[vmem] * len(inputs),
        scratch_shapes=[
            pltpu.VMEM(inputs[0].shape, BF16),
            pltpu.SemaphoreType.DMA((len(inputs),)),
        ],
        compiler_params=pltpu.CompilerParams(vmem_limit_bytes=58 * 1024 * 1024),
        cost_estimate=pl.CostEstimate(flops=0, bytes_accessed=9000000, transcendentals=0),
        name="fetch",
    )(*inputs)
    values = pl.pallas_call(
        functools.partial(evaluate_kernel, n_rows, n_blocks, locs),
        out_shape=jax.ShapeDtypeStruct((POWERS, places), F32),
        in_specs=[smem] + [smem] * n_blocks + [vmem] * (2 * n_blocks + 7),
        out_specs=vmem,
        scratch_shapes=[
            pltpu.VMEM((places, locs), jnp.int32),
            pltpu.VMEM((places, 2 * width + hidden_units), F32),
        ]
        + [
            pltpu.VMEM((rows, width), F32),
            pltpu.VMEM((rows, width), BF16),
            pltpu.VMEM((rows, 3 * width), BF16),
            pltpu.VMEM((rows, width), BF16),
            pltpu.VMEM((rows, width), BF16),
            pltpu.VMEM((rows, width), F32),
        ],
        compiler_params=pltpu.CompilerParams(vmem_limit_bytes=44 * 1024 * 1024),
        name="evaluate",
    )(send_load, *owners, *token_blocks, *actions, *held[:2], w_value.T, *held[2:], w_up, w_down)
    if n_rows == 2:
        shares = [values, lax.ppermute(values, "val", [(0, 1), (1, 0)])]
    else:
        shares = [lax.psum(values, "val")]
    chosen, counts, own_sums = pl.pallas_call(
        functools.partial(tally_kernel, n_rows, n_blocks),
        out_shape=(
            jax.ShapeDtypeStruct((places, LANES), jnp.int32),
            jax.ShapeDtypeStruct((ACTIONS, LANES), F32),
            jax.ShapeDtypeStruct((ACTIONS, LANES), F32),
        ),
        in_specs=[smem] + [vmem] * (2 * n_blocks + 1),
        out_specs=(vmem, vmem, vmem),
        scratch_shapes=[pltpu.VMEM((places, LANES), F32)],
        compiler_params=pltpu.CompilerParams(vmem_limit_bytes=16 * 1024 * 1024),
        cost_estimate=pl.CostEstimate(flops=0, bytes_accessed=4000000, transcendentals=0),
        name="tally",
    )(send_load, *owners, *actions, values)
    state_values, policy = pl.pallas_call(
        functools.partial(finish_kernel, n_rows, n_blocks),
        out_shape=(
            jax.ShapeDtypeStruct((POWERS, 1, slots), F32),
            jax.ShapeDtypeStruct((POWERS, boards, ACTIONS), F32),
        ),
        in_specs=[vmem] * (n_blocks + 3),
        out_specs=(vmem, vmem),
        scratch_shapes=[pltpu.VMEM((places, LANES), F32)],
        compiler_params=pltpu.CompilerParams(vmem_limit_bytes=16 * 1024 * 1024),
        name="finish",
    )(*shares, chosen, counts, own_sums)
    return (jnp.transpose(state_values, (1, 2, 0)), jnp.transpose(policy, (1, 0, 2)))


def solution(mesh):
    in_specs = (
        P(),
        P("val", "pos", None),
        P("val", "pos"),
        P("val", "pos", None),
        P("pos", None, None),
        P(),
        P(),
        P(),
        P(),
        P(),
        P(),
    )
    out_specs = (P("val", "pos", None), P("pos", None, None))
    return jax.shard_map(local, mesh=mesh, in_specs=in_specs, out_specs=out_specs, check_vma=False)
```

```python
import functools
import math

import jax
import jax.numpy as jnp
from jax import lax
from jax.experimental import pallas as pl
from jax.experimental.pallas import tpu as pltpu
from jax.sharding import PartitionSpec as P

HEADS = 8
POWERS = 7
ACTIONS = 32
ITERS = 8
SIZES = (8, 9, 10, 11, 12)
LANES = 128
PAD = 8
UNIT = 16
AHEAD = 8
SMOOTHING = 0.01
F32 = jnp.float32
BF16 = jnp.bfloat16


def dot(a, b):
    return jnp.dot(a, b, preferred_element_type=F32)


def dot_nt(a, b):
    return lax.dot_general(a, b, (((1,), (1,)), ((), ())), preferred_element_type=F32)


def dot_tn(a, b):
    return lax.dot_general(a, b, (((0,), (0,)), ((), ())), preferred_element_type=F32)


def norm(u):
    centre = u - jnp.mean(u, axis=-1, keepdims=True)
    spread = jnp.mean(centre * centre, axis=-1, keepdims=True)
    return centre * lax.rsqrt(spread + 1e-05)


def evaluate_kernel(n_rows, n_blocks, locs, *refs):
    load_ref = refs[0]
    owner_refs = refs[1 : 1 + n_blocks]
    token_refs = refs[1 + n_blocks : 1 + 2 * n_blocks]
    (
        board_ref,
        embed_ref,
        value_ref,
        qkv_ref,
        out_ref,
        up_ref,
        down_ref,
    ) = refs[1 + 3 * n_blocks : 8 + 3 * n_blocks]
    result_ref, token_ref, sum_ref = refs[8 + 3 * n_blocks : 11 + 3 * n_blocks]
    scratch = refs[11 + 3 * n_blocks :]
    pos, me = lax.axis_index("pos"), lax.axis_index("val")
    vocab, width = embed_ref.shape
    pitch = -(-locs // 16) * 16
    places = token_ref.shape[0]
    slots = places // n_rows
    starts, total = [], jnp.int32(0)
    for v in range(n_rows):
        starts.append(total)
        total = total + load_ref[v, pos]
    low = lax.div(me * total + (n_rows - 1), jnp.int32(n_rows))
    high = lax.div((me + 1) * total + (n_rows - 1), jnp.int32(n_rows))
    count = high - low

    def block_of(row):
        return lax.rem(row - me + n_rows, n_rows) if n_blocks == 2 else row

    def owner_at(block, slot):
        if n_blocks == 1:
            return owner_refs[0][block, slot]
        return jnp.where(block == 0, owner_refs[0][0, slot], owner_refs[1][0, slot])

    for b in range(n_blocks):
        part = places // n_blocks
        token_ref[b * part : (b + 1) * part, :] = token_refs[b][...]
    sum_ref[...] = jnp.zeros_like(sum_ref)
    gap = locs // 16 * 16
    for g in range(max(SIZES)):
        for r in scratch[:2]:
            blank = slice(g * pitch + gap, (g + 1) * pitch)
            r[blank] = jnp.zeros_like(r[blank])
    head = width // HEADS
    pair = 2 * head
    key_gap = jnp.zeros((LANES - pitch, pair), BF16)
    head_gap = jnp.zeros((head, LANES), BF16)
    first_half = lax.broadcasted_iota(jnp.int32, (pitch, pair), 1) < head
    first_scale = jnp.where(first_half, 1.0 / 128.0, 0.0).astype(BF16)
    second_scale = jnp.where(first_half, 0.0, 1.0 / 128.0).astype(BF16)
    row_k = lax.broadcasted_iota(jnp.int32, (2 * LANES, pair), 0)
    lane_k = lax.broadcasted_iota(jnp.int32, (2 * LANES, pair), 1)
    ones_block = jnp.where(
        (lax.rem(row_k, jnp.int32(LANES)) < locs) & ((row_k >= LANES) == (lane_k >= head)), 1.0, 0.0
    ).astype(BF16)
    score_scale = head ** (-0.5) * math.log2(math.e)
    selector_row = lax.broadcasted_iota(jnp.int32, (16, max(SIZES) * pitch), 0)
    selector_lane = lax.broadcasted_iota(jnp.int32, (16, max(SIZES) * pitch), 1)
    vocab_ids = lax.broadcasted_iota(jnp.int32, (vocab, locs), 0)

    def group_step(size, group, carry):
        first = group * size
        state_ref, exact_ref, joined_ref, mixed_ref, normed_ref, hidden_ref = scratch
        rows = slice(0, size * pitch)
        at = []
        selector = jnp.where(
            (lax.div(selector_lane, jnp.int32(pitch)) == selector_row)
            & (lax.rem(selector_lane, jnp.int32(pitch)) < locs),
            1.0,
            0.0,
        ).astype(BF16)[:, rows]

        def embed(g):
            item = low + jnp.minimum(first + g, count - 1)
            row, start = jnp.int32(0), jnp.int32(0)
            for v in range(1, n_rows):
                inside = item >= starts[v]
                row = jnp.where(inside, v, row)
                start = jnp.where(inside, starts[v], start)
            slot = item - start
            block = block_of(row)
            place = block * slots + slot
            at.append(place)
            board = lax.div(owner_at(block, slot), jnp.int32(ITERS))
            ids = token_ref[pl.ds(place, 1), :]
            hot = jnp.where(vocab_ids == ids, 1.0, 0.0).astype(BF16)
            exact = (dot_tn(hot, embed_ref[...]) + board_ref[board]).astype(BF16)
            exact_ref[g * pitch : g * pitch + locs, :] = exact
            state_ref[g * pitch : g * pitch + locs, :] = exact.astype(F32)

        def add_sums(lane, array):
            sums = dot(selector, array)
            for g in range(size):
                sum_ref[pl.ds(at[g], 1), lane : lane + sums.shape[1]] = sums[g : g + 1]

        def norm_state(g):
            here = slice(g * pitch, (g + 1) * pitch)
            normed_ref[here] = norm(state_ref[here]).astype(BF16)

        def join():
            joined_ref[rows] = dot(normed_ref[rows], qkv_ref[...]).astype(BF16)

        def score(g, p):
            here = slice(g * pitch, (g + 1) * pitch)
            lane = p * pair
            query = joined_ref[here, lane : lane + pair]
            key = joined_ref[here, width + lane : width + lane + pair]
            turned = jnp.concatenate([key, key_gap], axis=0).T
            keys = jnp.concatenate(
                [
                    jnp.concatenate([turned[:head], head_gap], axis=0),
                    jnp.concatenate([head_gap, turned[head:]], axis=0),
                ],
                axis=1,
            )
            return jnp.exp2(dot(query, keys) * score_scale).astype(BF16)

        def mix(g, p, weights):
            here = slice(g * pitch, (g + 1) * pitch)
            lane = p * pair
            value = joined_ref[here, 2 * width + lane : 2 * width + lane + pair]
            values = jnp.concatenate(
                [value * first_scale, key_gap, value * second_scale, key_gap], axis=0
            )
            both = dot(weights, jnp.concatenate([values, ones_block], axis=1))
            part = (both[:, :pair] / both[:, pair:] * 128.0).astype(BF16)
            mixed_ref[here, lane : lane + pair] = part

        def hide():
            hidden_ref[rows] = state_ref[rows] + dot(mixed_ref[rows], out_ref[...])

        def norm_hidden(g):
            here = slice(g * pitch, (g + 1) * pitch)
            normed_ref[here] = norm(hidden_ref[here]).astype(BF16)

        def feed():
            up = dot(normed_ref[rows], up_ref[...]).astype(BF16)
            inner = up * (
                jnp.asarray(math.sqrt(2.0 / math.pi), BF16)
                + jnp.asarray(math.sqrt(2.0 / math.pi) * 0.044715, BF16) * (up * up)
            )
            half = jnp.asarray(0.5, BF16) * up
            add_sums(2 * width, half + half * jnp.tanh(inner))

        for g in range(size):
            embed(g)
        for g in range(size):
            norm_state(g)
        join()
        order = [(g, p) for g in range(size) for p in range(HEADS // 2)]
        waiting = []
        for here in order + [None] * AHEAD:
            if here is not None:
                waiting.append((here, score(*here)))
            if here is None or len(waiting) > AHEAD:
                ready, weights = waiting.pop(0)
                mix(*ready, weights)
        hide()
        for g in range(size):
            norm_hidden(g)
        add_sums(0, exact_ref[rows])
        add_sums(width, mixed_ref[rows])
        feed()
        return carry

    below = 0
    for size in SIZES[1:]:
        fits = (count > below) & (count <= size)
        lax.fori_loop(0, jnp.where(fits, 1, 0), functools.partial(group_step, size), 0)
        below = size
    size = SIZES[0]
    steps = jnp.where(count > below, lax.div(count + (size - 1), jnp.int32(size)), 0)
    lax.fori_loop(0, steps, functools.partial(group_step, size), 0)
    mixed_active = sum_ref[:, width:]
    upper = mixed_active.astype(BF16)
    halves = jnp.concatenate([upper, (mixed_active - upper.astype(F32)).astype(BF16)], axis=0)
    added = dot(halves[:, :width], out_ref[...]) + dot(halves[:, width:], down_ref[...])
    final = sum_ref[:, :width] + (added[:places] + added[places:])
    pooled = norm(final * (1.0 / locs)).astype(BF16)
    raised = jnp.exp(2.0 * dot_nt(value_ref[...], pooled))
    values = raised / jnp.sum(raised, axis=0, keepdims=True)
    lane = lax.broadcasted_iota(jnp.int32, (POWERS, places), 1)
    mine = lane < 0
    for v in range(n_rows):
        slot = lane - block_of(v) * slots
        item = slot + starts[v]
        mine = mine | (
            (slot >= 0) & (slot < load_ref[v, pos]) & (item >= low) & (item < high)
        )
    result_ref[...] = jnp.where(mine, values, 0.0)


def fetch_kernel(n, *refs):
    sources = refs[:n]
    boards_ref, targets = refs[n], refs[n + 1 : 2 * n]
    board_ref, sem = refs[2 * n :]
    copies = [
        pltpu.make_async_copy(source, target, sem.at[i])
        for i, (source, target) in enumerate(zip(sources, (board_ref,) + targets))
    ]
    for copy in copies:
        copy.start()
    copies[0].wait()
    board = board_ref[...].astype(F32)
    for b in range(boards_ref.shape[0]):
        boards_ref[b] = board[:, b, :]
    for copy in copies[1:]:
        copy.wait()


def spread_powers(values):
    blank = jnp.zeros((PAD - values.shape[0], values.shape[1]), F32)
    turned = jnp.concatenate([values, blank], axis=0).T
    return jnp.concatenate([turned] * (LANES // PAD), axis=1)


def tally_kernel(n_rows, n_blocks, *refs):
    load_ref = refs[0]
    owner_refs = refs[1 : 1 + n_blocks]
    action_refs = refs[1 + n_blocks : 1 + 2 * n_blocks]
    value_ref, chosen_ref, count_ref, share_ref, spread_ref = refs[1 + 2 * n_blocks :]
    pos, me = lax.axis_index("pos"), lax.axis_index("val")
    places = chosen_ref.shape[0]
    slots = places // n_rows
    lane_cell = lax.div(lax.broadcasted_iota(jnp.int32, (slots, LANES), 1), jnp.int32(PAD))
    slot_down = lax.broadcasted_iota(jnp.int32, (slots, 1), 0)
    square = lax.broadcasted_iota(jnp.int32, (slots, slots), 0) == lax.broadcasted_iota(
        jnp.int32, (slots, slots), 1
    )
    if n_blocks == 2:
        spread_ref[...] = spread_powers(value_ref[...])
    for v in range(n_rows):
        if n_blocks == 1:
            row = jnp.int32(v)
            owners = owner_refs[0][v : v + 1, :]
            actions = [action_refs[0][i, v : v + 1, :] for i in range(POWERS)]
        else:
            row = lax.rem(me + v, n_rows)
            owners = owner_refs[v][...]
            actions = [action_refs[v][i] for i in range(POWERS)]
        cell = jnp.sum(jnp.where(square, owners, 0), axis=1, keepdims=True)
        spread = spread_powers(jnp.concatenate([a.astype(F32) for a in actions], axis=0))
        live = (lane_cell == cell) & (slot_down < load_ref[row, pos])
        chosen_ref[v * slots : (v + 1) * slots, :] = jnp.where(live, spread.astype(jnp.int32), -1)
    action_ids = lax.broadcasted_iota(jnp.int32, (ACTIONS, LANES), 0)

    def add_slots(step, sums):
        counts, shares = sums
        base = step * UNIT
        for k in range(UNIT):
            hit = action_ids == chosen_ref[pl.ds(base + k, 1), :]
            counts = counts + jnp.where(hit, 1.0, 0.0)
            if n_blocks == 2:
                shares = shares + jnp.where(hit, spread_ref[pl.ds(base + k, 1), :], 0.0)
        return counts, shares

    nothing = jnp.zeros((ACTIONS, LANES), F32)
    count_ref[...], share_ref[...] = over_slots(places, add_slots, (nothing, nothing))


def over_slots(places, add_slots, sums):
    if places > 2 * UNIT:
        return lax.fori_loop(0, places // UNIT, add_slots, sums)
    for step in range(places // UNIT):
        sums = add_slots(step, sums)
    return sums


def finish_kernel(n_rows, n_blocks, *refs):
    value_refs = refs[:n_blocks]
    chosen_ref, count_ref, share_ref, state_values_ref, policy_ref, spread_ref = refs[n_blocks:]
    slots = state_values_ref.shape[2]
    boards = policy_ref.shape[1]
    places = chosen_ref.shape[0]
    arrived = value_refs[-1][...]
    if n_blocks == 2:
        values = value_refs[0][:, :slots] + arrived[:, slots:]
        spread = spread_powers(arrived)
        spread_ref[:slots] = spread[slots:]
        spread_ref[slots:] = spread[:slots]
    else:
        me = lax.axis_index("val")
        values = arrived[:, :slots]
        for v in range(1, n_rows):
            values = jnp.where(me == v, arrived[:, v * slots : (v + 1) * slots], values)
        spread_ref[...] = spread_powers(arrived)
    for i in range(POWERS):
        state_values_ref[i] = values[i : i + 1]
    action_ids = lax.broadcasted_iota(jnp.int32, (ACTIONS, LANES), 0)

    def add_slots(step, sums):
        base = step * UNIT
        for k in range(UNIT):
            hit = action_ids == chosen_ref[pl.ds(base + k, 1), :]
            sums = sums + jnp.where(hit, spread_ref[pl.ds(base + k, 1), :], 0.0)
        return sums

    counts = count_ref[...]
    value_sums = over_slots(places, add_slots, share_ref[...])
    visits = jnp.sum(counts, axis=0, keepdims=True)
    totals = jnp.sum(value_sums, axis=0, keepdims=True)
    baseline = (totals + 1.0 / POWERS) / (visits + 1.0)
    payoff = (value_sums + baseline) / (counts + 1.0)
    payoffs = [payoff] + [pltpu.roll(payoff, LANES - t * PAD, 1) for t in range(1, ITERS)]
    smoothed = [SMOOTHING * jnp.sum(current, axis=0, keepdims=True) for current in payoffs]
    regrets = jnp.zeros((ACTIONS, LANES), F32)
    average = jnp.zeros((ACTIONS, LANES), F32)
    for t in range(ITERS):
        current = payoffs[t]
        positive = jnp.maximum(regrets, 0.0)
        weight = 1.0 / (jnp.sum(positive, axis=0, keepdims=True) + ACTIONS * SMOOTHING)
        expected = jnp.sum(positive * current, axis=0, keepdims=True) + smoothed[t]
        average = average + (positive + SMOOTHING) * weight
        regrets = regrets + current - expected * weight
    turned = (average / ITERS).T
    for b in range(boards):
        first = b * ITERS * PAD
        policy_ref[:, b, :] = turned[first : first + POWERS]


def local(
    send_load,
    tokens,
    owner,
    joint_action,
    board_context,
    tok_embed,
    w_qkv,
    w_attn_out,
    w_up,
    w_down,
    w_value,
):
    n_rows = lax.axis_size("val")
    slots, locs = tokens.shape[1:]
    boards = board_context.shape[0]
    width, hidden_units = w_up.shape
    tokens = tokens.reshape(slots, locs)
    actions = jnp.transpose(joint_action, (2, 0, 1))
    if n_rows == 2:

        def rows_of(array, axis):
            return [array, lax.ppermute(array, "val", [(0, 1), (1, 0)])]

    else:

        def rows_of(array, axis):
            return [lax.all_gather(array, "val", axis=axis, tiled=True)]

    token_blocks, owners, actions = rows_of(tokens, 0), rows_of(owner, 0), rows_of(actions, 1)
    n_blocks = len(owners)
    vmem = pl.BlockSpec(memory_space=pltpu.VMEM)
    smem = pl.BlockSpec(memory_space=pltpu.SMEM)
    hbm = pl.BlockSpec(memory_space=pl.ANY)
    rows = max(SIZES) * (-(-locs // 16) * 16)
    places = n_rows * slots
    inputs = (jnp.transpose(board_context, (1, 0, 2)), w_qkv, w_attn_out)
    held = pl.pallas_call(
        functools.partial(fetch_kernel, len(inputs)),
        out_shape=[pltpu.VMEM((boards, locs, width), F32)]
        + [pltpu.VMEM(w.shape, BF16) for w in inputs[1:]],
        in_specs=[hbm] * len(inputs),
        out_specs=[vmem] * len(inputs),
        scratch_shapes=[
            pltpu.VMEM(inputs[0].shape, BF16),
            pltpu.SemaphoreType.DMA((len(inputs),)),
        ],
        compiler_params=pltpu.CompilerParams(vmem_limit_bytes=58 * 1024 * 1024),
        cost_estimate=pl.CostEstimate(flops=0, bytes_accessed=9000000, transcendentals=0),
        name="fetch",
    )(*inputs)
    values = pl.pallas_call(
        functools.partial(evaluate_kernel, n_rows, n_blocks, locs),
        out_shape=jax.ShapeDtypeStruct((POWERS, places), F32),
        in_specs=[smem] + [smem] * n_blocks + [vmem] * (2 * n_blocks + 7),
        out_specs=vmem,
        scratch_shapes=[
            pltpu.VMEM((places, locs), jnp.int32),
            pltpu.VMEM((places, 2 * width + hidden_units), F32),
        ]
        + [
            pltpu.VMEM((rows, width), F32),
            pltpu.VMEM((rows, width), BF16),
            pltpu.VMEM((rows, 3 * width), BF16),
            pltpu.VMEM((rows, width), BF16),
            pltpu.VMEM((rows, width), BF16),
            pltpu.VMEM((rows, width), F32),
        ],
        compiler_params=pltpu.CompilerParams(vmem_limit_bytes=44 * 1024 * 1024),
        name="evaluate",
    )(send_load, *owners, *token_blocks, *actions, held[0], tok_embed, w_value.T, *held[1:], w_up, w_down)
    if n_rows == 2:
        shares = [values, lax.ppermute(values, "val", [(0, 1), (1, 0)])]
    else:
        shares = [lax.psum(values, "val")]
    chosen, counts, own_sums = pl.pallas_call(
        functools.partial(tally_kernel, n_rows, n_blocks),
        out_shape=(
            jax.ShapeDtypeStruct((places, LANES), jnp.int32),
            jax.ShapeDtypeStruct((ACTIONS, LANES), F32),
            jax.ShapeDtypeStruct((ACTIONS, LANES), F32),
        ),
        in_specs=[smem] + [vmem] * (2 * n_blocks + 1),
        out_specs=(vmem, vmem, vmem),
        scratch_shapes=[pltpu.VMEM((places, LANES), F32)],
        compiler_params=pltpu.CompilerParams(vmem_limit_bytes=16 * 1024 * 1024),
        cost_estimate=pl.CostEstimate(flops=0, bytes_accessed=4000000, transcendentals=0),
        name="tally",
    )(send_load, *owners, *actions, values)
    state_values, policy = pl.pallas_call(
        functools.partial(finish_kernel, n_rows, n_blocks),
        out_shape=(
            jax.ShapeDtypeStruct((POWERS, 1, slots), F32),
            jax.ShapeDtypeStruct((POWERS, boards, ACTIONS), F32),
        ),
        in_specs=[vmem] * (n_blocks + 3),
        out_specs=(vmem, vmem),
        scratch_shapes=[pltpu.VMEM((places, LANES), F32)],
        compiler_params=pltpu.CompilerParams(vmem_limit_bytes=16 * 1024 * 1024),
        name="finish",
    )(*shares, chosen, counts, own_sums)
    return (jnp.transpose(state_values, (1, 2, 0)), jnp.transpose(policy, (1, 0, 2)))


def solution(mesh):
    in_specs = (
        P(),
        P("val", "pos", None),
        P("val", "pos"),
        P("val", "pos", None),
        P("pos", None, None),
        P(),
        P(),
        P(),
        P(),
        P(),
        P(),
    )
    out_specs = (P("val", "pos", None), P("pos", None, None))
    return jax.shard_map(local, mesh=mesh, in_specs=in_specs, out_specs=out_specs, check_vma=False)
```

```python
import functools
import math

import jax
import jax.numpy as jnp
from jax import lax
from jax.experimental import pallas as pl
from jax.experimental.pallas import tpu as pltpu
from jax.sharding import PartitionSpec as P

HEADS = 8
POWERS = 7
ACTIONS = 32
ITERS = 8
SIZES = (7, 8, 9, 10, 11, 12)
LANES = 128
PAD = 8
UNIT = 16
AHEAD = 8
SMOOTHING = 0.01
F32 = jnp.float32
BF16 = jnp.bfloat16


def dot(a, b):
    return jnp.dot(a, b, preferred_element_type=F32)


def dot_nt(a, b):
    return lax.dot_general(a, b, (((1,), (1,)), ((), ())), preferred_element_type=F32)


def dot_tn(a, b):
    return lax.dot_general(a, b, (((0,), (0,)), ((), ())), preferred_element_type=F32)


def norm(u):
    centre = u - jnp.mean(u, axis=-1, keepdims=True)
    spread = jnp.mean(centre * centre, axis=-1, keepdims=True)
    return centre * lax.rsqrt(spread + 1e-05)


def evaluate_kernel(n_rows, n_blocks, locs, *refs):
    load_ref = refs[0]
    owner_refs = refs[1 : 1 + n_blocks]
    token_refs = refs[1 + n_blocks : 1 + 2 * n_blocks]
    (
        board_ref,
        embed_ref,
        value_ref,
        qkv_ref,
        out_ref,
        up_ref,
        down_ref,
    ) = refs[1 + 3 * n_blocks : 8 + 3 * n_blocks]
    result_ref, token_ref, sum_ref = refs[8 + 3 * n_blocks : 11 + 3 * n_blocks]
    scratch = refs[11 + 3 * n_blocks :]
    pos, me = lax.axis_index("pos"), lax.axis_index("val")
    vocab, width = embed_ref.shape
    pitch = -(-locs // 16) * 16
    places = token_ref.shape[0]
    slots = places // n_rows
    starts, total = [], jnp.int32(0)
    for v in range(n_rows):
        starts.append(total)
        total = total + load_ref[v, pos]
    low = lax.div(me * total + (n_rows - 1), jnp.int32(n_rows))
    high = lax.div((me + 1) * total + (n_rows - 1), jnp.int32(n_rows))
    count = high - low

    def block_of(row):
        return lax.rem(row - me + n_rows, n_rows) if n_blocks == 2 else row

    def owner_at(block, slot):
        if n_blocks == 1:
            return owner_refs[0][block, slot]
        return jnp.where(block == 0, owner_refs[0][0, slot], owner_refs[1][0, slot])

    for b in range(n_blocks):
        part = places // n_blocks
        token_ref[b * part : (b + 1) * part, :] = token_refs[b][...]
    sum_ref[...] = jnp.zeros_like(sum_ref)
    gap = locs // 16 * 16
    for g in range(max(SIZES)):
        for r in scratch[:2]:
            blank = slice(g * pitch + gap, (g + 1) * pitch)
            r[blank] = jnp.zeros_like(r[blank])
    head = width // HEADS
    pair = 2 * head
    key_gap = jnp.zeros((LANES - pitch, pair), BF16)
    head_gap = jnp.zeros((head, LANES), BF16)
    first_half = lax.broadcasted_iota(jnp.int32, (pitch, pair), 1) < head
    first_scale = jnp.where(first_half, 1.0 / 128.0, 0.0).astype(BF16)
    second_scale = jnp.where(first_half, 0.0, 1.0 / 128.0).astype(BF16)
    row_k = lax.broadcasted_iota(jnp.int32, (2 * LANES, pair), 0)
    lane_k = lax.broadcasted_iota(jnp.int32, (2 * LANES, pair), 1)
    ones_block = jnp.where(
        (lax.rem(row_k, jnp.int32(LANES)) < locs) & ((row_k >= LANES) == (lane_k >= head)), 1.0, 0.0
    ).astype(BF16)
    score_scale = head ** (-0.5) * math.log2(math.e)
    selector_row = lax.broadcasted_iota(jnp.int32, (16, max(SIZES) * pitch), 0)
    selector_lane = lax.broadcasted_iota(jnp.int32, (16, max(SIZES) * pitch), 1)
    vocab_ids = lax.broadcasted_iota(jnp.int32, (vocab, locs), 0)

    def group_step(size, group, carry):
        first = group * size
        state_ref, exact_ref, joined_ref, mixed_ref, normed_ref, hidden_ref = scratch
        rows = slice(0, size * pitch)
        at = []
        selector = jnp.where(
            (lax.div(selector_lane, jnp.int32(pitch)) == selector_row)
            & (lax.rem(selector_lane, jnp.int32(pitch)) < locs),
            1.0,
            0.0,
        ).astype(BF16)[:, rows]

        def embed(g):
            item = low + jnp.minimum(first + g, count - 1)
            row, start = jnp.int32(0), jnp.int32(0)
            for v in range(1, n_rows):
                inside = item >= starts[v]
                row = jnp.where(inside, v, row)
                start = jnp.where(inside, starts[v], start)
            slot = item - start
            block = block_of(row)
            place = block * slots + slot
            at.append(place)
            board = lax.div(owner_at(block, slot), jnp.int32(ITERS))
            ids = token_ref[pl.ds(place, 1), :]
            hot = jnp.where(vocab_ids == ids, 1.0, 0.0).astype(BF16)
            exact = (dot_tn(hot, embed_ref[...]) + board_ref[board]).astype(BF16)
            exact_ref[g * pitch : g * pitch + locs, :] = exact
            state_ref[g * pitch : g * pitch + locs, :] = exact.astype(F32)

        def add_sums(lane, array):
            sums = dot(selector, array)
            for g in range(size):
                sum_ref[pl.ds(at[g], 1), lane : lane + sums.shape[1]] = sums[g : g + 1]

        def norm_state(g):
            here = slice(g * pitch, (g + 1) * pitch)
            normed_ref[here] = norm(state_ref[here]).astype(BF16)

        def join():
            joined_ref[rows] = dot(normed_ref[rows], qkv_ref[...]).astype(BF16)

        def score(g, p):
            here = slice(g * pitch, (g + 1) * pitch)
            lane = p * pair
            query = joined_ref[here, lane : lane + pair]
            key = joined_ref[here, width + lane : width + lane + pair]
            turned = jnp.concatenate([key, key_gap], axis=0).T
            keys = jnp.concatenate(
                [
                    jnp.concatenate([turned[:head], head_gap], axis=0),
                    jnp.concatenate([head_gap, turned[head:]], axis=0),
                ],
                axis=1,
            )
            return jnp.exp2(dot(query, keys) * score_scale).astype(BF16)

        def mix(g, p, weights):
            here = slice(g * pitch, (g + 1) * pitch)
            lane = p * pair
            value = joined_ref[here, 2 * width + lane : 2 * width + lane + pair]
            values = jnp.concatenate(
                [value * first_scale, key_gap, value * second_scale, key_gap], axis=0
            )
            both = dot(weights, jnp.concatenate([values, ones_block], axis=1))
            part = (both[:, :pair] / both[:, pair:] * 128.0).astype(BF16)
            mixed_ref[here, lane : lane + pair] = part

        def hide():
            hidden_ref[rows] = state_ref[rows] + dot(mixed_ref[rows], out_ref[...])

        def norm_hidden(g):
            here = slice(g * pitch, (g + 1) * pitch)
            normed_ref[here] = norm(hidden_ref[here]).astype(BF16)

        def feed():
            up = dot(normed_ref[rows], up_ref[...]).astype(BF16)
            inner = up * (
                jnp.asarray(math.sqrt(2.0 / math.pi), BF16)
                + jnp.asarray(math.sqrt(2.0 / math.pi) * 0.044715, BF16) * (up * up)
            )
            half = jnp.asarray(0.5, BF16) * up
            add_sums(2 * width, half + half * jnp.tanh(inner))

        for g in range(size):
            embed(g)
        for g in range(size):
            norm_state(g)
        join()
        order = [(g, p) for g in range(size) for p in range(HEADS // 2)]
        waiting = []
        for here in order + [None] * AHEAD:
            if here is not None:
                waiting.append((here, score(*here)))
            if here is None or len(waiting) > AHEAD:
                ready, weights = waiting.pop(0)
                mix(*ready, weights)
        hide()
        for g in range(size):
            norm_hidden(g)
        add_sums(0, exact_ref[rows])
        add_sums(width, mixed_ref[rows])
        feed()
        return carry

    below = 0
    small, large = SIZES[:2]
    for size in SIZES[2:]:
        fits = (count > below) & (count <= size)
        lax.fori_loop(0, jnp.where(fits, 1, 0), functools.partial(group_step, size), 0)
        below = size
    steps = jnp.where(count > below, lax.div(count + (large - 1), jnp.int32(large)), 0)
    short = steps * small >= count
    for size, chosen in ((small, short), (large, jnp.logical_not(short))):
        lax.fori_loop(0, jnp.where(chosen, steps, 0), functools.partial(group_step, size), 0)
    mixed_active = sum_ref[:, width:]
    upper = mixed_active.astype(BF16)
    halves = jnp.concatenate([upper, (mixed_active - upper.astype(F32)).astype(BF16)], axis=0)
    added = dot(halves[:, :width], out_ref[...]) + dot(halves[:, width:], down_ref[...])
    final = sum_ref[:, :width] + (added[:places] + added[places:])
    pooled = norm(final * (1.0 / locs)).astype(BF16)
    raised = jnp.exp(2.0 * dot_nt(value_ref[...], pooled))
    values = raised / jnp.sum(raised, axis=0, keepdims=True)
    lane = lax.broadcasted_iota(jnp.int32, (POWERS, places), 1)
    mine = lane < 0
    for v in range(n_rows):
        slot = lane - block_of(v) * slots
        item = slot + starts[v]
        mine = mine | (
            (slot >= 0) & (slot < load_ref[v, pos]) & (item >= low) & (item < high)
        )
    result_ref[...] = jnp.where(mine, values, 0.0)


def fetch_kernel(n, *refs):
    sources = refs[:n]
    boards_ref, targets = refs[n], refs[n + 1 : 2 * n]
    board_ref, sem = refs[2 * n :]
    copies = [
        pltpu.make_async_copy(source, target, sem.at[i])
        for i, (source, target) in enumerate(zip(sources, (board_ref,) + targets))
    ]
    for copy in copies:
        copy.start()
    copies[0].wait()
    board = board_ref[...].astype(F32)
    for b in range(boards_ref.shape[0]):
        boards_ref[b] = board[:, b, :]
    for copy in copies[1:]:
        copy.wait()


def spread_powers(values):
    blank = jnp.zeros((PAD - values.shape[0], values.shape[1]), F32)
    turned = jnp.concatenate([values, blank], axis=0).T
    return jnp.concatenate([turned] * (LANES // PAD), axis=1)


def tally_kernel(n_rows, n_blocks, *refs):
    load_ref = refs[0]
    owner_refs = refs[1 : 1 + n_blocks]
    action_refs = refs[1 + n_blocks : 1 + 2 * n_blocks]
    value_ref, chosen_ref, count_ref, share_ref, spread_ref = refs[1 + 2 * n_blocks :]
    pos, me = lax.axis_index("pos"), lax.axis_index("val")
    places = chosen_ref.shape[0]
    slots = places // n_rows
    lane_cell = lax.div(lax.broadcasted_iota(jnp.int32, (slots, LANES), 1), jnp.int32(PAD))
    slot_down = lax.broadcasted_iota(jnp.int32, (slots, 1), 0)
    square = lax.broadcasted_iota(jnp.int32, (slots, slots), 0) == lax.broadcasted_iota(
        jnp.int32, (slots, slots), 1
    )
    if n_blocks == 2:
        spread_ref[...] = spread_powers(value_ref[...])
    for v in range(n_rows):
        if n_blocks == 1:
            row = jnp.int32(v)
            owners = owner_refs[0][v : v + 1, :]
            actions = [action_refs[0][i, v : v + 1, :] for i in range(POWERS)]
        else:
            row = lax.rem(me + v, n_rows)
            owners = owner_refs[v][...]
            actions = [action_refs[v][i] for i in range(POWERS)]
        cell = jnp.sum(jnp.where(square, owners, 0), axis=1, keepdims=True)
        spread = spread_powers(jnp.concatenate([a.astype(F32) for a in actions], axis=0))
        live = (lane_cell == cell) & (slot_down < load_ref[row, pos])
        chosen_ref[v * slots : (v + 1) * slots, :] = jnp.where(live, spread.astype(jnp.int32), -1)
    action_ids = lax.broadcasted_iota(jnp.int32, (ACTIONS, LANES), 0)

    def add_slots(step, sums):
        counts, shares = sums
        base = step * UNIT
        for k in range(UNIT):
            hit = action_ids == chosen_ref[pl.ds(base + k, 1), :]
            counts = counts + jnp.where(hit, 1.0, 0.0)
            if n_blocks == 2:
                shares = shares + jnp.where(hit, spread_ref[pl.ds(base + k, 1), :], 0.0)
        return counts, shares

    nothing = jnp.zeros((ACTIONS, LANES), F32)
    count_ref[...], share_ref[...] = over_slots(places, add_slots, (nothing, nothing))


def over_slots(places, add_slots, sums):
    if places > 2 * UNIT:
        return lax.fori_loop(0, places // UNIT, add_slots, sums)
    for step in range(places // UNIT):
        sums = add_slots(step, sums)
    return sums


def finish_kernel(n_rows, n_blocks, *refs):
    value_refs = refs[:n_blocks]
    chosen_ref, count_ref, share_ref, state_values_ref, policy_ref, spread_ref = refs[n_blocks:]
    slots = state_values_ref.shape[2]
    boards = policy_ref.shape[1]
    places = chosen_ref.shape[0]
    arrived = value_refs[-1][...]
    if n_blocks == 2:
        values = value_refs[0][:, :slots] + arrived[:, slots:]
        spread = spread_powers(arrived)
        spread_ref[:slots] = spread[slots:]
        spread_ref[slots:] = spread[:slots]
    else:
        me = lax.axis_index("val")
        values = arrived[:, :slots]
        for v in range(1, n_rows):
            values = jnp.where(me == v, arrived[:, v * slots : (v + 1) * slots], values)
        spread_ref[...] = spread_powers(arrived)
    for i in range(POWERS):
        state_values_ref[i] = values[i : i + 1]
    action_ids = lax.broadcasted_iota(jnp.int32, (ACTIONS, LANES), 0)

    def add_slots(step, sums):
        base = step * UNIT
        for k in range(UNIT):
            hit = action_ids == chosen_ref[pl.ds(base + k, 1), :]
            sums = sums + jnp.where(hit, spread_ref[pl.ds(base + k, 1), :], 0.0)
        return sums

    counts = count_ref[...]
    value_sums = over_slots(places, add_slots, share_ref[...])
    visits = jnp.sum(counts, axis=0, keepdims=True)
    totals = jnp.sum(value_sums, axis=0, keepdims=True)
    baseline = (totals + 1.0 / POWERS) / (visits + 1.0)
    payoff = (value_sums + baseline) / (counts + 1.0)
    payoffs = [payoff] + [pltpu.roll(payoff, LANES - t * PAD, 1) for t in range(1, ITERS)]
    smoothed = [SMOOTHING * jnp.sum(current, axis=0, keepdims=True) for current in payoffs]
    regrets = jnp.zeros((ACTIONS, LANES), F32)
    average = jnp.zeros((ACTIONS, LANES), F32)
    for t in range(ITERS):
        current = payoffs[t]
        positive = jnp.maximum(regrets, 0.0)
        weight = 1.0 / (jnp.sum(positive, axis=0, keepdims=True) + ACTIONS * SMOOTHING)
        expected = jnp.sum(positive * current, axis=0, keepdims=True) + smoothed[t]
        average = average + (positive + SMOOTHING) * weight
        regrets = regrets + current - expected * weight
    turned = (average / ITERS).T
    for b in range(boards):
        first = b * ITERS * PAD
        policy_ref[:, b, :] = turned[first : first + POWERS]


def local(
    send_load,
    tokens,
    owner,
    joint_action,
    board_context,
    tok_embed,
    w_qkv,
    w_attn_out,
    w_up,
    w_down,
    w_value,
):
    n_rows = lax.axis_size("val")
    slots, locs = tokens.shape[1:]
    boards = board_context.shape[0]
    width, hidden_units = w_up.shape
    tokens = tokens.reshape(slots, locs)
    actions = jnp.transpose(joint_action, (2, 0, 1))
    if n_rows == 2:

        def rows_of(array, axis):
            return [array, lax.ppermute(array, "val", [(0, 1), (1, 0)])]

    else:

        def rows_of(array, axis):
            return [lax.all_gather(array, "val", axis=axis, tiled=True)]

    token_blocks, owners, actions = rows_of(tokens, 0), rows_of(owner, 0), rows_of(actions, 1)
    n_blocks = len(owners)
    vmem = pl.BlockSpec(memory_space=pltpu.VMEM)
    smem = pl.BlockSpec(memory_space=pltpu.SMEM)
    hbm = pl.BlockSpec(memory_space=pl.ANY)
    rows = max(SIZES) * (-(-locs // 16) * 16)
    places = n_rows * slots
    inputs = (jnp.transpose(board_context, (1, 0, 2)), w_qkv, w_attn_out)
    held = pl.pallas_call(
        functools.partial(fetch_kernel, len(inputs)),
        out_shape=[pltpu.VMEM((boards, locs, width), F32)]
        + [pltpu.VMEM(w.shape, BF16) for w in inputs[1:]],
        in_specs=[hbm] * len(inputs),
        out_specs=[vmem] * len(inputs),
        scratch_shapes=[
            pltpu.VMEM(inputs[0].shape, BF16),
            pltpu.SemaphoreType.DMA((len(inputs),)),
        ],
        compiler_params=pltpu.CompilerParams(vmem_limit_bytes=58 * 1024 * 1024),
        cost_estimate=pl.CostEstimate(flops=0, bytes_accessed=9000000, transcendentals=0),
        name="fetch",
    )(*inputs)
    values = pl.pallas_call(
        functools.partial(evaluate_kernel, n_rows, n_blocks, locs),
        out_shape=jax.ShapeDtypeStruct((POWERS, places), F32),
        in_specs=[smem] + [smem] * n_blocks + [vmem] * (2 * n_blocks + 7),
        out_specs=vmem,
        scratch_shapes=[
            pltpu.VMEM((places, locs), jnp.int32),
            pltpu.VMEM((places, 2 * width + hidden_units), F32),
        ]
        + [
            pltpu.VMEM((rows, width), F32),
            pltpu.VMEM((rows, width), BF16),
            pltpu.VMEM((rows, 3 * width), BF16),
            pltpu.VMEM((rows, width), BF16),
            pltpu.VMEM((rows, width), BF16),
            pltpu.VMEM((rows, width), F32),
        ],
        compiler_params=pltpu.CompilerParams(vmem_limit_bytes=44 * 1024 * 1024),
        name="evaluate",
    )(send_load, *owners, *token_blocks, *actions, held[0], tok_embed, w_value.T, *held[1:], w_up, w_down)
    if n_rows == 2:
        shares = [values, lax.ppermute(values, "val", [(0, 1), (1, 0)])]
    else:
        shares = [lax.psum(values, "val")]
    chosen, counts, own_sums = pl.pallas_call(
        functools.partial(tally_kernel, n_rows, n_blocks),
        out_shape=(
            jax.ShapeDtypeStruct((places, LANES), jnp.int32),
            jax.ShapeDtypeStruct((ACTIONS, LANES), F32),
            jax.ShapeDtypeStruct((ACTIONS, LANES), F32),
        ),
        in_specs=[smem] + [vmem] * (2 * n_blocks + 1),
        out_specs=(vmem, vmem, vmem),
        scratch_shapes=[pltpu.VMEM((places, LANES), F32)],
        compiler_params=pltpu.CompilerParams(vmem_limit_bytes=16 * 1024 * 1024),
        cost_estimate=pl.CostEstimate(flops=0, bytes_accessed=4000000, transcendentals=0),
        name="tally",
    )(send_load, *owners, *actions, values)
    state_values, policy = pl.pallas_call(
        functools.partial(finish_kernel, n_rows, n_blocks),
        out_shape=(
            jax.ShapeDtypeStruct((POWERS, 1, slots), F32),
            jax.ShapeDtypeStruct((POWERS, boards, ACTIONS), F32),
        ),
        in_specs=[vmem] * (n_blocks + 3),
        out_specs=(vmem, vmem),
        scratch_shapes=[pltpu.VMEM((places, LANES), F32)],
        compiler_params=pltpu.CompilerParams(vmem_limit_bytes=16 * 1024 * 1024),
        name="finish",
    )(*shares, chosen, counts, own_sums)
    return (jnp.transpose(state_values, (1, 2, 0)), jnp.transpose(policy, (1, 0, 2)))


def solution(mesh):
    in_specs = (
        P(),
        P("val", "pos", None),
        P("val", "pos"),
        P("val", "pos", None),
        P("pos", None, None),
        P(),
        P(),
        P(),
        P(),
        P(),
        P(),
    )
    out_specs = (P("val", "pos", None), P("pos", None, None))
    return jax.shard_map(local, mesh=mesh, in_specs=in_specs, out_specs=out_specs, check_vma=False)
```
